128 devices in a mesh: rep: 8 (over y, x_hi), fsdp: 16 (over z, x_lo, core).
Axes of the slice: x: 4 (x_hi: 2, x_lo: 2; x = x_hi * 2 + x_lo), y: 4, z: 4, core: 2. Of those that a mesh axis runs over, the one named last changes fastest.
Arguments:
- hidden: bfloat16 [8, 4096, 8192], P('rep', 'fsdp'), may hold values from -6 to 6
- replay_buffer: bfloat16 [8, 2048, 8192], P('rep', 'fsdp'), may hold values from -6 to 6
- replay_index: int32 [8, 1024], P('rep', 'fsdp'), may hold values from 0 to 127, as said below
- cotangent: bfloat16 [8, 5120, 1024], P('rep', 'fsdp'), may hold values from -8 to 8
- norm_gain: bfloat16 [8192], replicated, may hold values from 0.3 to 2.4
- value_weight: bfloat16 [8, 8192, 1024], P('rep', 'fsdp'), may hold values from -0.0625 to 0.0625
- adam_first: float32 [8, 8192, 1024], P('rep', 'fsdp'), may hold values from -0.0014648438 to 0.0014648438
- adam_second: float32 [8, 8192, 1024], P('rep', 'fsdp'), may hold values from 1.1920929e-08 to 2.3841858e-07
- anchor: float32 [8192, 1024], P('fsdp', 'rep'), may hold values from -0.0625 to 0.0625
- outer_momentum: float32 [8192, 1024], P('fsdp', 'rep'), may hold values from -0.078125 to 0.078125
Outputs:
- input_grad: bfloat16 [8, 5120, 8192], P('rep', 'fsdp')
- first_moment: float32 [8, 8192, 1024], P('rep', 'fsdp')
- second_moment: float32 [8, 8192, 1024], P('rep', 'fsdp')
- synced_weight: bfloat16 [8192, 1024], P('fsdp')
- new_momentum: float32 [8192, 1024], P('fsdp', 'rep')
- new_anchor: float32 [8192, 1024], P('fsdp', 'rep')
The draws below stay inside these ranges and needn't reach their ends.
Inputs may be any that keep to these rules, and one draw needn't show every extreme that they name: `replay_index`: each entry names a row of the own block of 128 rows of the device that holds it; both 0 and 127 occur among every device's entries.
All inputs are finite; a program needn't handle non-finite values.
Results may differ from the reference program's by a relative error of at most 0.015.
Values may be sent and summed in bfloat16 or wider, within the bound.
No kernel may reach another device: no remote copies, remote signals or barrier semaphores. Data moves between devices by JAX's collectives and lax.ppermute only.
A program may use at most 128 MiB of HBM per device.

```python
import math
import jax
import jax.numpy as jnp
from jax import lax

D = 8192
KV = 1024
TOK_DEV = 256
BUF_DEV = 128
RPL_DEV = 64
ROWS_DEV = 320
TOKENS = 4096
BUF = 2048
ROWS = 5120
N_REP = 8
N_FSDP = 16


def draw_replay_index(key, part):
    key = jax.random.fold_in(key, 11)
    key_values, key_place = jax.random.split(key)
    values = jax.random.randint(key_values, (N_REP, N_FSDP, RPL_DEV), 0, BUF_DEV)
    place_high = jax.random.randint(key_place, (N_REP, N_FSDP, 1), 0, RPL_DEV)
    place_low = (place_high + 1) % RPL_DEV
    position = jnp.arange(RPL_DEV)[None, None, :]
    values = jnp.where(position == place_high, BUF_DEV - 1, jnp.where(position == place_low, 0, values))
    return values.reshape(N_REP, N_FSDP * RPL_DEV).astype(jnp.int32)


def draw_cotangent(key, part):
    key = jax.random.fold_in(key, 23)
    key_base = jax.random.fold_in(key, 0)
    total_rows = N_FSDP * (TOK_DEV + RPL_DEV)
    ramp = 0.5 + 1.5 * jnp.arange(total_rows, dtype=jnp.float32) / total_rows
    ramp = ramp[None, :, None]
    base = jnp.clip(jax.random.normal(key_base, (N_REP, total_rows, KV), jnp.float32), -4.0, 4.0)
    values = base * ramp
    return jnp.clip(values, -8.0, 8.0).astype(jnp.bfloat16)


def draw_norm_gain(key, part):
    key = jax.random.fold_in(key, 31)
    place = jnp.arange(D, dtype=jnp.float32) / (D - 1)
    ramp = 0.5 + place
    rough = jax.random.uniform(key, (D,), jnp.float32, 0.8, 1.2)
    return (ramp * rough).astype(jnp.bfloat16)


def spiked(drawn, own_key, source, target, shards_of, factor):
    owner, partner = [(jnp.arange(drawn.shape[dim]) // (drawn.shape[dim] // shards_of)).reshape([-1 if axis == dim else 1 for axis in range(drawn.ndim)]) for dim in (source, target)]
    chosen = jax.random.permutation(own_key, shards_of)[partner]
    strong = (owner == chosen) | (owner == (partner + shards_of // 2) % shards_of)
    return jnp.where(strong, factor * drawn, drawn)


def block_levels(stream_key, dims, cuts, low, high):
    def one(axis_at, parts):
        steps = jax.random.uniform(jax.random.fold_in(jax.random.fold_in(stream_key, 6), axis_at), (parts,), jnp.float32, low / len(cuts), high / len(cuts))
        return jnp.repeat(jnp.exp(steps), dims[axis_at] // parts).reshape((-1,) + (1,) * (len(dims) - axis_at - 1))

    factor_of = one(*cuts[0])
    for cut in cuts[1:]:
        factor_of = factor_of * one(*cut)
    return factor_of


def bell_draw(stream_key, shape, width, reach, cuts=(), held_as=jnp.bfloat16):
    values = width * jax.random.normal(stream_key, shape, jnp.float32)
    if cuts:
        values = values * block_levels(stream_key, shape, cuts, -0.22, 0.18)
    return jnp.clip(values, -reach, reach).astype(held_as)


def bell_draw_with(key, shape, spread, reach, shards, heavy, kind=jnp.bfloat16):
    result = spread * jax.random.normal(key, shape, jnp.float32)
    if shards:
        result = result * block_levels(key, shape, shards, -0.22, 0.18)
    return jnp.clip(spiked(result, jax.random.fold_in(key, 3), *heavy), -reach, reach).astype(kind)


def setup_inputs(seed: int = 0) -> dict:
    arg_keys = jax.random.split(jax.random.key(seed), 11)
    hidden = bell_draw_with(arg_keys[0], (N_REP, TOKENS, D), 1.0, 6.0, ((0, 8), (1, 16)), (1, 2, 16, 2.0))
    replay_buffer = bell_draw(arg_keys[1], (N_REP, BUF, D), 1.0, 6.0, ((0, 8), (1, 16)))
    replay_index = draw_replay_index(jax.random.fold_in(arg_keys[10], 71), 0)
    cotangent = draw_cotangent(jax.random.fold_in(arg_keys[10], 71), 0)
    norm_gain = draw_norm_gain(jax.random.fold_in(arg_keys[10], 71), 0)
    value_weight = bell_draw(arg_keys[5], (N_REP, D, KV), D ** -0.5, 0.0625, ((0, 8), (1, 16)))
    adam_first = bell_draw(arg_keys[6], (N_REP, D, KV), (0.3 * (D * KV) ** -0.5), 0.0014648438, ((0, 8), (1, 16)), jnp.float32)
    adam_second = jnp.clip(jnp.exp(math.log(2.384185791015625e-07) - 2.9957323 * jax.random.uniform(arg_keys[7], (N_REP, D, KV), jnp.float32) ** block_levels(arg_keys[7], (N_REP, D, KV), ((0, 8), (1, 16)), -0.2, 0.2)), 1.1920929132713809e-08, 2.384185791015625e-07)
    anchor = bell_draw(arg_keys[8], (D, KV), D ** -0.5, 0.0625, ((0, 16), (1, 8)), jnp.float32)
    outer_momentum = bell_draw(arg_keys[9], (D, KV), 0.005, 0.078125, ((0, 16), (1, 8)), jnp.float32)
    return dict(hidden=hidden, replay_buffer=replay_buffer, replay_index=replay_index, cotangent=cotangent, norm_gain=norm_gain, value_weight=value_weight, adam_first=adam_first, adam_second=adam_second, anchor=anchor, outer_momentum=outer_momentum)


norm_eps = 1e-05
adam_eps = 1e-08
inner_rate = 0.01
first_decay = 0.9
second_decay = 0.95
clip_limit = 1.0
outer_beta = 0.9
outer_rate = 0.7
replay_weight = 0.5

def one_replica(packed, norm_gain):
    fresh, buffer_rows, picks, cot_rows, weight, first_in, second_in = packed
    fresh_blocks = fresh.reshape(N_FSDP, TOK_DEV, D)
    buffer_blocks = buffer_rows.reshape(N_FSDP, BUF_DEV, D)
    pick_blocks = picks.reshape(N_FSDP, RPL_DEV).astype(jnp.int32)
    replayed = jax.vmap(lambda block, index: jnp.take(block, index, axis=0))(buffer_blocks, pick_blocks)
    row_data = jnp.concatenate([fresh_blocks, replayed], axis=1)
    row_float = row_data.astype(jnp.float32)
    inv_rms = lax.rsqrt(lax.optimization_barrier(jnp.mean(row_float * row_float, axis=-1, keepdims=True)) + norm_eps)
    normed = row_float * inv_rms
    gain_float = norm_gain.astype(jnp.float32)
    normed_in = (normed * gain_float).astype(jnp.bfloat16)
    row_scale = jnp.where(jnp.arange(ROWS_DEV) < TOK_DEV, 1.0, replay_weight).astype(jnp.bfloat16)
    scaled_cot = cot_rows.reshape(N_FSDP, ROWS_DEV, KV) * row_scale[None, :, None]

    def add_partial(total, pair):
        left, right = pair
        partial_term = lax.dot_general(left, right, (((0,), (0,)), ((), ())), preferred_element_type=jnp.float32)
        rounded = lax.optimization_barrier(partial_term.astype(jnp.bfloat16))
        return (total + rounded.astype(jnp.float32), None)
    grad, _ = lax.scan(add_partial, jnp.zeros((D, KV), jnp.float32), (normed_in, scaled_cot))
    clip_factor = jnp.minimum(1.0, clip_limit / jnp.sqrt(jnp.sum(grad * grad)))
    clipped = grad * clip_factor
    first = first_decay * first_in + (1.0 - first_decay) * clipped
    second = second_decay * second_in + (1.0 - second_decay) * clipped * clipped
    inner_new = (weight.astype(jnp.float32) - inner_rate * first / (jnp.sqrt(second) + adam_eps)).astype(jnp.bfloat16)
    flat_cot = scaled_cot.reshape(ROWS, KV)
    normed_grad = lax.dot_general(flat_cot, weight, (((1,), (1,)), ((), ())), preferred_element_type=jnp.float32)
    normed_grad = lax.optimization_barrier(normed_grad.astype(jnp.bfloat16)).astype(jnp.float32)
    flat_normed = normed.reshape(ROWS, D)
    flat_inv = inv_rms.reshape(ROWS, 1)
    gained = gain_float * normed_grad
    inner_mean = lax.optimization_barrier(jnp.mean(flat_normed * gained, axis=-1, keepdims=True))
    input_grad = (flat_inv * (gained - flat_normed * inner_mean)).astype(jnp.bfloat16)
    return (inner_new, input_grad, first, second)

def reference(hidden, replay_buffer, replay_index, cotangent, norm_gain, value_weight, adam_first, adam_second, anchor, outer_momentum):
    inner_all, input_grad, first_moment, second_moment = lax.map(lambda packed: one_replica(packed, norm_gain), (hidden, replay_buffer, replay_index, cotangent, value_weight, adam_first, adam_second))
    inner_total = lax.optimization_barrier(jnp.sum(inner_all.astype(jnp.float32), axis=0))
    outer_grad = anchor - inner_total / N_REP
    new_momentum = outer_beta * outer_momentum + outer_grad
    new_anchor = anchor - outer_rate * (outer_grad + outer_beta * new_momentum)
    synced_weight = new_anchor.astype(jnp.bfloat16)
    return (input_grad, first_moment, second_moment, synced_weight, new_momentum, new_anchor)
```

```python
import functools

import jax
import jax.numpy as jnp
from jax import lax
from jax.experimental import pallas as pl
from jax.experimental.pallas import tpu as pltpu
from jax.sharding import PartitionSpec as P

norm_eps = 1e-05
adam_eps = 1e-08
inner_rate = 0.01
first_decay = 0.9
second_decay = 0.95
clip_limit = 1.0
outer_beta = 0.9
outer_rate = 0.7
replay_weight = 0.5

F32 = jnp.float32
BF16 = jnp.bfloat16
MIB = 1024 * 1024


def sds(shape, dtype):
    return jax.ShapeDtypeStruct(shape, dtype)


def cost(flops, size):
    return pl.CostEstimate(flops=int(flops), bytes_accessed=int(size), transcendentals=0)


def params(mib):
    return pltpu.CompilerParams(vmem_limit_bytes=mib * MIB)


def clip_index(t, start, count):
    return jnp.clip(t - start, 0, count - 1)


def over_core(value):
    return lax.ppermute(value, "fsdp", [(i, i ^ 1) for i in range(16)])


def over_x(value):
    return lax.ppermute(value, "fsdp", [(i, i ^ 2) for i in range(16)])


def over_z(value, step):
    return lax.ppermute(value, "fsdp", [(i, (i + 4 * step) % 16) for i in range(16)])


def over_x_hi(value):
    return lax.ppermute(value, "rep", [(i, i ^ 1) for i in range(8)])


def over_y(value, step):
    return lax.ppermute(value, "rep", [(i, (i + 2 * step) % 8) for i in range(8)])


def lane_sum(value):
    total = value[:, 0:128]
    for at in range(128, value.shape[1], 128):
        total = total + value[:, at : at + 128]
    return total


def prep_kernel(core_ref, index_ref, hk_ref, hs_ref, bk_ref, bs_ref, cot_ref, xk_ref, xs_ref, cp_ref, inv_ref, total_ref):
    step = pl.program_id(0)
    rows = lax.broadcasted_iota(jnp.int32, (128, 64), 0)
    pick = jnp.where(rows == index_ref[...], 1.0, 0.0).astype(BF16)
    squares = jnp.zeros((320, 128), F32)
    for h_ref, b_ref, x_ref in ((hk_ref, bk_ref, xk_ref), (hs_ref, bs_ref, xs_ref)):
        replayed = lax.dot_general(pick, b_ref[...], (((0,), (0,)), ((), ())), preferred_element_type=F32)
        fresh = h_ref[...]
        x_ref[0:256, :] = fresh
        x_ref[256:320, :] = replayed.astype(BF16)
        fresh = fresh.astype(F32)
        squares = squares + jnp.concatenate([lane_sum(fresh * fresh), lane_sum(replayed * replayed)], axis=0)

    @pl.when(step == 0)
    def _():
        total_ref[...] = squares

    @pl.when(step > 0)
    def _():
        total_ref[...] += squares

    @pl.when(step == 7)
    def _():
        mean = jnp.sum(total_ref[...], axis=1, keepdims=True) / 8192.0
        inv = lax.rsqrt(mean + norm_eps)
        inv_ref[...] = jnp.broadcast_to(inv, (320, 128))
        at = lax.broadcasted_iota(jnp.int32, (320, 1), 0)
        scale = inv * jnp.where(at < 256, 1.0, replay_weight)
        cp_ref[...] = (cot_ref[...].astype(F32) * scale).astype(BF16)


def prep(core, hidden, replay_buffer, replay_index, cotangent):
    def block(rows, flip):
        return pl.BlockSpec((None, rows, 512), lambda g, c: (0, 0, 2 * g + ((1 - c[0]) if flip else c[0])))

    return pl.pallas_call(
        prep_kernel,
        grid_spec=pltpu.PrefetchScalarGridSpec(
            num_scalar_prefetch=1,
            grid=(8,),
            in_specs=[
                pl.BlockSpec((1, 64), lambda g, c: (0, 0)),
                block(256, False),
                block(256, True),
                block(128, False),
                block(128, True),
                pl.BlockSpec((None, 320, 1024), lambda g, c: (0, 0, 0)),
            ],
            out_specs=[
                pl.BlockSpec((None, 320, 512), lambda g, c: (g, 0, 0)),
                pl.BlockSpec((None, 320, 512), lambda g, c: (g, 0, 0)),
                pl.BlockSpec((320, 1024), lambda g, c: (0, 0)),
                pl.BlockSpec((320, 128), lambda g, c: (0, 0)),
            ],
            scratch_shapes=[pltpu.VMEM((320, 128), F32)],
        ),
        out_shape=[
            sds((8, 320, 512), BF16),
            sds((8, 320, 512), BF16),
            sds((320, 1024), BF16),
            sds((320, 128), F32),
        ],
        compiler_params=params(32),
        cost_estimate=cost(2e9, 12e6),
        name="prep",
    )(core, replay_index, hidden, hidden, replay_buffer, replay_buffer, cotangent)


def grad_kernel(runs, table_ref, xk_ref, xs_ref, c_ref, cs_ref, *rest):
    outs, (x_all, c_all) = rest[:-2], rest[-2:]
    step = pl.program_id(0)

    @pl.when(step == 0)
    def _():
        c_all[0:320, :] = c_ref[...]
        c_all[320:640, :] = cs_ref[...]

    x_all[0:320, :] = xk_ref[...]
    x_all[320:640, :] = xs_ref[...]
    part = lax.dot_general(x_all[...], c_all[...], (((0,), (0,)), ((), ())), preferred_element_type=F32).astype(BF16)
    for out_ref, (start, count) in zip(outs, runs):

        @pl.when((step >= start) & (step < start + count))
        def _(out_ref=out_ref):
            out_ref[...] = part


def grad_blocks(place, outputs, xk, xs, c, cs, name):
    z, x = place
    blocks = [b for out in outputs for b in out]
    table = jnp.stack([jnp.stack([((z + dz) % 4) * 2 + (x ^ dx), jnp.int32(h)]) for dz, dx, h in blocks])
    runs, start = [], 0
    for out in outputs:
        runs.append((start, len(out)))
        start += len(out)
    x_spec = pl.BlockSpec((None, 320, 256), lambda t, tab: (tab[t, 0], 0, tab[t, 1]))
    c_spec = pl.BlockSpec((320, 1024), lambda t, tab: (0, 0))
    return pl.pallas_call(
        functools.partial(grad_kernel, runs),
        grid_spec=pltpu.PrefetchScalarGridSpec(
            num_scalar_prefetch=1,
            grid=(len(blocks),),
            in_specs=[x_spec, x_spec, c_spec, c_spec],
            out_specs=[
                pl.BlockSpec((None, 256, 1024), lambda t, tab, s=s, n=n: (clip_index(t, s, n), 0, 0)) for s, n in runs
            ],
            scratch_shapes=[pltpu.VMEM((640, 256), BF16), pltpu.VMEM((640, 1024), BF16)],
        ),
        out_shape=[sds((n, 256, 1024), BF16) for _, n in runs],
        compiler_params=params(48),
        cost_estimate=cost(len(blocks) * 2 * 640 * 256 * 1024, len(blocks) * 900e3),
        name=name,
    )(table, xk, xs, c, cs)


def total_kernel(a0, a1, a2, a3, b0, b1, gain_ref, grad_ref, sq_ref):
    step = pl.program_id(0)
    top = (a0[...].astype(F32) + a1[...].astype(F32)) + (a2[...].astype(F32) + a3[...].astype(F32))
    low = b0[...].astype(F32) + b1[...].astype(F32)
    top = top * gain_ref[0:256, :]
    low = low * gain_ref[256:512, :]
    grad_ref[0:256, :] = top
    grad_ref[256:512, :] = low
    both = lane_sum(top * top + low * low)
    square = jnp.sum(both.reshape(32, 8, 128), axis=0)

    @pl.when(step == 0)
    def _():
        sq_ref[...] = square

    @pl.when(step > 0)
    def _():
        sq_ref[...] += square


def total(a0, a1, a2, a3, b0, b1, gain_rows):
    part = pl.BlockSpec((256, 256), lambda t: (0, t))
    return pl.pallas_call(
        total_kernel,
        grid=(4,),
        in_specs=[part] * 6 + [pl.BlockSpec((512, 1), lambda t: (0, 0))],
        out_specs=[pl.BlockSpec((512, 256), lambda t: (0, t)), pl.BlockSpec((8, 128), lambda t: (0, 0))],
        out_shape=[sds((512, 1024), F32), sds((8, 128), F32)],
        compiler_params=params(32),
        cost_estimate=cost(5e6, 5e6),
        name="total",
    )(a0, a1, a2, a3, b0, b1, gain_rows)


def adam_kernel(table_ref, sq_ref, grad_ref, m_ref, v_ref, w_ref, first_ref, second_ref, *outs):
    step = pl.program_id(0)
    squares = jnp.sum(sq_ref[...], axis=1, keepdims=True)
    squares = jnp.sum(squares, axis=0, keepdims=True)
    factor = jnp.minimum(1.0, clip_limit / jnp.sqrt(squares))
    clipped = grad_ref[...] * factor
    first = first_decay * m_ref[...] + (1.0 - first_decay) * clipped
    second = second_decay * v_ref[...] + (1.0 - second_decay) * clipped * clipped
    first_ref[...] = first
    second_ref[...] = second
    new = w_ref[...].astype(F32) - inner_rate * first / (jnp.sqrt(second) + adam_eps)
    new = new.astype(BF16)
    for k, out_ref in enumerate(outs):

        @pl.when((step >= 2 * k) & (step < 2 * k + 2))
        def _(out_ref=out_ref):
            out_ref[...] = new


def adam(table, sq, grad, first_in, second_in, weight):
    column = pl.BlockSpec((512, 128), lambda t, tab: (0, tab[t]))
    lead = pl.BlockSpec((None, 512, 128), lambda t, tab: (0, 0, tab[t]))
    return pl.pallas_call(
        adam_kernel,
        grid_spec=pltpu.PrefetchScalarGridSpec(
            num_scalar_prefetch=1,
            grid=(8,),
            in_specs=[pl.BlockSpec((8, 128), lambda t, tab: (0, 0)), column, lead, lead, lead],
            out_specs=[lead, lead]
            + [pl.BlockSpec((None, 512, 128), lambda t, tab, k=k: (clip_index(t, 2 * k, 2), 0, 0)) for k in range(4)],
        ),
        out_shape=[sds((1, 512, 1024), F32)] * 2 + [sds((2, 512, 128), BF16)] * 4,
        compiler_params=params(32),
        cost_estimate=cost(2e7, 12e6),
        name="adam",
    )(table, sq, grad, first_in, second_in, weight)


def place_kernel(table_ref, *refs):
    step = pl.program_id(0)
    for k, in_ref in enumerate(refs[:-1]):

        @pl.when((step >= 2 * k) & (step < 2 * k + 2))
        def _(in_ref=in_ref):
            refs[-1][...] = in_ref[...]


def place_columns(table, parts):
    return pl.pallas_call(
        place_kernel,
        grid_spec=pltpu.PrefetchScalarGridSpec(
            num_scalar_prefetch=1,
            grid=(8,),
            in_specs=[
                pl.BlockSpec((None, 512, 128), lambda t, tab, k=k: (clip_index(t, 2 * k, 2), 0, 0)) for k in range(4)
            ],
            out_specs=pl.BlockSpec((512, 128), lambda t, tab: (0, tab[t])),
        ),
        out_shape=sds((512, 1024), BF16),
        compiler_params=params(32),
        cost_estimate=cost(1e6, 2e6),
        name="place",
    )(table, *parts)


def input_kernel(groups, table_ref, xk_ref, xs_ref, cp_ref, inv_ref, gain_ref, *rest):
    weights = rest[: len(groups)]
    out_ref, q_ref, m_ref = rest[len(groups) :]
    step = pl.program_id(0)
    n_q = sum(count for _, count, _, _ in groups)

    @pl.when(step == 0)
    def _():
        m_ref[...] = jnp.zeros_like(m_ref)

    for w_ref, (start, count, sibling, half) in zip(weights, groups):

        @pl.when((step >= start) & (step < start + count))
        def _(w_ref=w_ref, sibling=sibling, half=half):
            q = lax.dot_general(cp_ref[...], w_ref[...], (((1,), (1,)), ((), ())), preferred_element_type=F32)
            g = table_ref[step]
            columns = slice(256 * half, 256 * half + 256)
            gain = gain_ref[2 * g + (table_ref[64] ^ sibling)][:, columns].astype(F32)
            gained = q * gain
            x = (xs_ref if sibling else xk_ref)[...]
            m_ref[...] += lane_sum(gained * x[:, columns].astype(F32))
            q_ref[sibling * 8 + g, :, columns] = gained.astype(BF16)

    for sibling in range(2):

        @pl.when((step >= n_q + 8 * sibling) & (step < n_q + 8 * sibling + 8))
        def _(sibling=sibling):
            g = table_ref[step]
            inv = inv_ref[:, 0:1]
            factor = jnp.sum(m_ref[...], axis=1, keepdims=True) * (inv * inv) / 8192.0
            x = (xs_ref if sibling else xk_ref)[...].astype(F32)
            out_ref[...] = (q_ref[sibling * 8 + g].astype(F32) - x * factor).astype(BF16)


def input_gradient(core, place, xk, xs, cp, inv, gain, weights):
    z, x = place
    groups, order, start = [], [], 0
    for array, sibling, half, chunks in weights:
        groups.append((start, len(chunks), sibling, half))
        order += [((z + dz) % 4) * 2 + (x ^ dx) for dz, dx in chunks]
        start += len(chunks)
    n_q, n_mine = start, start // 2
    order += [jnp.int32(g) for g in range(8)] * 2
    order += [jnp.int32(0)] * (64 - len(order)) + [core]
    table = jnp.stack(order)

    def mine(t, tab):
        at = jnp.where(t < n_mine, t, jnp.where(t < n_q, n_mine - 1, jnp.clip(t, n_q, n_q + 7)))
        return (tab[at], 0, 0)

    def theirs(t, tab):
        at = jnp.where(t < n_q, jnp.clip(t, n_mine, n_q - 1), jnp.where(t < n_q + 8, n_q - 1, t))
        return (tab[at], 0, 0)

    def out_at(t, tab):
        g = tab[jnp.maximum(t, n_q)]
        return (0, 0, 2 * g + (tab[64] ^ jnp.where(t < n_q + 8, 0, 1)))

    return pl.pallas_call(
        functools.partial(input_kernel, groups),
        grid_spec=pltpu.PrefetchScalarGridSpec(
            num_scalar_prefetch=1,
            grid=(n_q + 16,),
            in_specs=[
                pl.BlockSpec((None, 320, 512), mine),
                pl.BlockSpec((None, 320, 512), theirs),
                pl.BlockSpec((320, 1024), lambda t, tab: (0, 0)),
                pl.BlockSpec((320, 128), lambda t, tab: (0, 0)),
                pl.BlockSpec((16, 1, 512), lambda t, tab: (0, 0, 0)),
            ]
            + [
                pl.BlockSpec((None, 256, 1024), lambda t, tab, s=s, n=n: (clip_index(t, s, n), 0, 0))
                for s, n, _, _ in groups
            ],
            out_specs=pl.BlockSpec((None, 320, 512), out_at),
            scratch_shapes=[pltpu.VMEM((16, 320, 512), BF16), pltpu.VMEM((320, 128), F32)],
        ),
        out_shape=sds((1, 320, 8192), BF16),
        compiler_params=params(56),
        cost_estimate=cost(6e9, 40e6),
        name="input_gradient",
    )(table, xk, xs, cp, inv, gain, *[w[0] for w in weights])


def add(*values):
    total_value = values[0].astype(F32)
    for value in values[1:]:
        total_value = total_value + value.astype(F32)
    return total_value.astype(BF16)


def on_device(
    hidden,
    replay_buffer,
    replay_index,
    cotangent,
    norm_gain,
    value_weight,
    adam_first,
    adam_second,
    anchor,
    outer_momentum,
):
    fsdp = lax.axis_index("fsdp")
    rep = lax.axis_index("rep")
    core, x, z = fsdp % 2, (fsdp // 2) % 2, fsdp // 4
    x_hi, y = rep % 2, rep // 2
    place = (z, x)
    columns = jnp.stack([((y + dy) % 4) * 2 + (x_hi ^ dx) for dy in range(4) for dx in range(2)])
    gain_float = norm_gain.astype(F32)

    w0, w1 = value_weight[0, 0:256], value_weight[0, 256:512]
    wx = over_x(w0)
    u_m = over_z(w1, 1)
    u_p = over_z(w1, -1)

    xk, xs, cp, inv = prep(core[None], hidden, replay_buffer, replay_index, cotangent)
    x_sib = over_core(xs)
    c_sib = over_core(cp)

    b_up, b_down, a_send, a_last = grad_blocks(
        place,
        [[(2, 0, 1)], [(2, 1, 1)], [(2, 1, 0), (1, 1, 0), (3, 1, 0)], [(0, 1, 0)]],
        xk, x_sib, cp, c_sib, "grad_a",
    )
    r_up = over_z(b_up, 1)
    r_down = over_z(b_down, -1)
    r_a = over_x(a_send)
    b_10, b_11, b_30, b_31, a_own, b_0 = grad_blocks(
        place,
        [[(1, 0, 1)], [(1, 1, 1)], [(3, 0, 1)], [(3, 1, 1)], [(2, 0, 0), (1, 0, 0), (3, 0, 0), (0, 0, 0)], [(0, 0, 1), (0, 1, 1)]],
        xk, x_sib, cp, c_sib, "grad_b",
    )
    e_up = over_z(b_11, 1)
    e_down = over_z(b_30, -1)
    r_a_last = over_x(a_last)
    l_up = over_z(add(b_10, r_up), 1)
    l_down = over_z(add(b_31, r_down), -1)

    s_2 = add(a_own[0], r_a[0])
    s_1 = add(a_own[1], r_a[1])
    s_3 = add(a_own[2], r_a[2])
    p_up = over_z(s_2[0:128], 1)
    p_down = over_z(s_2[128:256], -1)
    b_mine = add(b_0[0], l_up[0], e_down[0])
    b_theirs = add(b_0[1], e_up[0], l_down[0])
    r_b = over_x(b_theirs)
    s_1 = jnp.concatenate([add(s_1[0:128], p_up), s_1[128:256]], axis=0)
    s_3 = jnp.concatenate([s_3[0:128], add(s_3[128:256], p_down)], axis=0)
    f_up = over_z(s_1, 1)
    f_down = over_z(s_3, -1)

    gain_rows = lax.dynamic_slice(gain_float, (fsdp * 512,), (512,))[:, None]
    grad, squares = total(a_own[3], r_a_last[0], f_up, f_down, b_mine, r_b, gain_rows)

    squares = squares + over_core(squares)
    squares = squares + over_x(squares)
    squares = squares + over_z(squares, 1)
    squares = squares + over_z(squares, 2)

    first, second, n_0, n_1, n_2, n_3 = adam(columns, squares, grad, adam_first, adam_second, value_weight)

    v_up = over_z(u_m[0:128], 1)
    v_down = over_z(u_p[128:256], -1)
    zf = jnp.stack([w1, u_p, jnp.concatenate([v_up, v_down], axis=0), u_m])
    zfx = over_x(zf)
    pair = jnp.stack([w0, wx])
    pair_m = over_z(pair, 1)
    pair_p = over_z(pair, -1)
    pair_2a = over_z(pair_m[0:1], 1)
    pair_2b = over_z(pair_p[1:2], -1)
    xf_order = [(0, 0), (0, 1)]
    gathered = [
        (pair, 0, [(0, 0), (0, 1)]),
        (zf, 1, [(dz, 0) for dz in range(4)]),
        (pair_m, 0, [(3, 0), (3, 1)]),
        (pair_p, 0, [(1, 0), (1, 1)]),
        (pair_2a, 0, [(2, 0)]),
        (pair_2b, 0, [(2, 1)]),
        (zfx, 1, [(dz, 1) for dz in range(4)]),
    ]
    weights = [(array, 0, half, chunks) for array, half, chunks in gathered]
    weights += [(over_core(array), 1, half, chunks) for array, half, chunks in gathered]
    input_grad = input_gradient(
        core, place, xk, xs, cp, inv, gain_float.reshape(16, 1, 512), weights
    )

    m_1 = over_y(n_1, 1)
    m_2 = over_y(n_2, 2)
    m_3 = over_y(n_3, 3)
    summed = n_0.astype(F32) + m_1.astype(F32) + m_2.astype(F32) + m_3.astype(F32)
    inner_total = summed[0] + over_x_hi(summed[1].astype(BF16)).astype(F32)
    outer_grad = anchor - inner_total / 8
    new_momentum = outer_beta * outer_momentum + outer_grad
    new_anchor = anchor - outer_rate * (outer_grad + outer_beta * new_momentum)
    sent = new_anchor.astype(BF16)
    sent = jnp.stack([sent, over_x_hi(sent)])
    parts = [sent, over_y(sent, 3), over_y(sent, 2), over_y(sent, 1)]
    synced_weight = place_columns(columns, parts)
    return (input_grad, first, second, synced_weight, new_momentum, new_anchor)


def solution(mesh):
    return jax.shard_map(
        on_device,
        mesh=mesh,
        in_specs=(
            P("rep", "fsdp", None),
            P("rep", "fsdp", None),
            P("rep", "fsdp"),
            P("rep", "fsdp", None),
            P(),
            P("rep", "fsdp", None),
            P("rep", "fsdp", None),
            P("rep", "fsdp", None),
            P("fsdp", "rep"),
            P("fsdp", "rep"),
        ),
        out_specs=(
            P("rep", "fsdp", None),
            P("rep", "fsdp", None),
            P("rep", "fsdp", None),
            P("fsdp", None),
            P("fsdp", "rep"),
            P("fsdp", "rep"),
        ),
        check_vma=False,
    )
```

```python
import functools

import jax
import jax.numpy as jnp
from jax import lax
from jax.experimental import pallas as pl
from jax.experimental.pallas import tpu as pltpu
from jax.sharding import PartitionSpec as P

norm_eps = 1e-05
adam_eps = 1e-08
inner_rate = 0.01
first_decay = 0.9
second_decay = 0.95
clip_limit = 1.0
outer_beta = 0.9
outer_rate = 0.7
replay_weight = 0.5

F32 = jnp.float32
BF16 = jnp.bfloat16
MIB = 1024 * 1024


def sds(shape, dtype):
    return jax.ShapeDtypeStruct(shape, dtype)


def cost(flops, size):
    return pl.CostEstimate(flops=int(flops), bytes_accessed=int(size), transcendentals=0)


def params(mib):
    return pltpu.CompilerParams(vmem_limit_bytes=mib * MIB)


def clip_index(t, start, count):
    return jnp.clip(t - start, 0, count - 1)


def over_core(value):
    return lax.ppermute(value, "fsdp", [(i, i ^ 1) for i in range(16)])


def over_x(value):
    return lax.ppermute(value, "fsdp", [(i, i ^ 2) for i in range(16)])


def over_z(value, step):
    return lax.ppermute(value, "fsdp", [(i, (i + 4 * step) % 16) for i in range(16)])


def over_x_hi(value):
    return lax.ppermute(value, "rep", [(i, i ^ 1) for i in range(8)])


def over_y(value, step):
    return lax.ppermute(value, "rep", [(i, (i + 2 * step) % 8) for i in range(8)])


def lane_sum(value):
    total = value[:, 0:128]
    for at in range(128, value.shape[1], 128):
        total = total + value[:, at : at + 128]
    return total


def prep_kernel(core_ref, index_ref, h_ref, b_ref, cot_ref, xk_ref, xs_ref, cp_ref, inv_ref, total_ref):
    step = pl.program_id(0)
    core = core_ref[0]
    rows = lax.broadcasted_iota(jnp.int32, (128, 64), 0)
    pick = jnp.where(rows == index_ref[...], 1.0, 0.0).astype(BF16)
    squares = jnp.zeros((320, 128), F32)
    for j in range(2):
        for flip, x_ref in ((0, xk_ref), (1, xs_ref)):
            columns = pl.ds(pl.multiple_of(1024 * j + 512 * (core ^ flip), 512), 512)
            replayed = lax.dot_general(pick, b_ref[:, columns], (((0,), (0,)), ((), ())), preferred_element_type=F32)
            fresh = h_ref[:, columns]
            x_ref[j, 0:256, :] = fresh
            x_ref[j, 256:320, :] = replayed.astype(BF16)
            fresh = fresh.astype(F32)
            squares = squares + jnp.concatenate([lane_sum(fresh * fresh), lane_sum(replayed * replayed)], axis=0)

    @pl.when(step == 0)
    def _():
        total_ref[...] = squares

    @pl.when(step > 0)
    def _():
        total_ref[...] += squares

    @pl.when(step == 3)
    def _():
        mean = jnp.sum(total_ref[...], axis=1, keepdims=True) / 8192.0
        inv = lax.rsqrt(mean + norm_eps)
        inv_ref[...] = jnp.broadcast_to(inv, (320, 128))
        at = lax.broadcasted_iota(jnp.int32, (320, 1), 0)
        scale = inv * jnp.where(at < 256, 1.0, replay_weight)
        cp_ref[...] = (cot_ref[...].astype(F32) * scale).astype(BF16)


def prep(core, hidden, replay_buffer, replay_index, cotangent):
    return pl.pallas_call(
        prep_kernel,
        grid_spec=pltpu.PrefetchScalarGridSpec(
            num_scalar_prefetch=1,
            grid=(4,),
            in_specs=[
                pl.BlockSpec((1, 64), lambda t, c: (0, 0)),
                pl.BlockSpec((None, 256, 2048), lambda t, c: (0, 0, t)),
                pl.BlockSpec((None, 128, 2048), lambda t, c: (0, 0, t)),
                pl.BlockSpec((None, 320, 1024), lambda t, c: (0, 0, 0)),
            ],
            out_specs=[
                pl.BlockSpec((2, 320, 512), lambda t, c: (t, 0, 0)),
                pl.BlockSpec((2, 320, 512), lambda t, c: (t, 0, 0)),
                pl.BlockSpec((320, 1024), lambda t, c: (0, 0)),
                pl.BlockSpec((320, 128), lambda t, c: (0, 0)),
            ],
            scratch_shapes=[pltpu.VMEM((320, 128), F32)],
        ),
        out_shape=[
            sds((8, 320, 512), BF16),
            sds((8, 320, 512), BF16),
            sds((320, 1024), BF16),
            sds((320, 128), F32),
        ],
        compiler_params=params(60),
        cost_estimate=cost(2e9, 12e6),
        name="prep",
    )(core, replay_index, hidden, replay_buffer, cotangent)


x_first = 448
z_first = 1024 - x_first


def grad_kernel(plan, table_ref, xk_ref, xs_ref, c_ref, cs_ref, *rest):
    outs, (x_all, c_all) = rest[:-2], rest[-2:]
    step = pl.program_id(0)
    x = table_ref[4]

    @pl.when(step == 0)
    def _():
        c_all[:, 0:320] = c_ref[...].T
        c_all[:, 320:640] = cs_ref[...].T

    for dx in range(2):
        x_all[0:320, 512 * dx : 512 * dx + 512] = xk_ref[x ^ dx]
        x_all[320:640, 512 * dx : 512 * dx + 512] = xs_ref[x ^ dx]
    for at in range(max(start + count for _, _, start, count in plan)):

        @pl.when(step == at)
        def _(at=at):
            for low in range(2):
                rows = c_all[0:x_first, :] if low else c_all[x_first:1024, :]
                part = jnp.dot(rows, x_all[...], preferred_element_type=F32).astype(BF16)
                for out_ref, (out_low, dx, start, count) in zip(outs, plan):
                    if out_low == low and start <= at < start + count:
                        out_ref[...] = part[:, 512 * dx : 512 * dx + 512]


def grad_blocks(place, chunks, outputs, xk, xs, c, cs, name):
    z, x = place
    table = jnp.stack([(z + dz) % 4 for dz in chunks] + [jnp.int32(0)] * (4 - len(chunks)) + [x])
    x_spec = pl.BlockSpec((2, 320, 512), lambda t, tab: (tab[t], 0, 0))
    c_spec = pl.BlockSpec((320, 1024), lambda t, tab: (0, 0))
    return pl.pallas_call(
        functools.partial(grad_kernel, outputs),
        grid_spec=pltpu.PrefetchScalarGridSpec(
            num_scalar_prefetch=1,
            grid=(len(chunks),),
            in_specs=[x_spec, x_spec, c_spec, c_spec],
            out_specs=[
                pl.BlockSpec(
                    (None, x_first if low else z_first, 512), lambda t, tab, s=s, n=n: (clip_index(t, s, n), 0, 0)
                )
                for low, _, s, n in outputs
            ],
            scratch_shapes=[pltpu.VMEM((640, 1024), BF16), pltpu.VMEM((1024, 640), BF16)],
        ),
        out_shape=[sds((n, x_first if low else z_first, 512), BF16) for low, _, _, n in outputs],
        compiler_params=params(60),
        cost_estimate=cost(len(chunks) * 2 * 640 * 1024 * 1024, len(chunks) * 3.4e6),
        name=name,
    )(table, xk, xs, c, cs)


early_rows = 128


def total_kernel(a0, a1, ue, ul, de, dl, b0, b1, gain_ref, w_ref, grad_ref, sq_ref, late_ref):
    step = pl.program_id(0)
    late_ref[...] = w_ref[early_rows:512, :]
    up = jnp.concatenate([ul[...], ue[...]], axis=0).astype(F32)
    down = jnp.concatenate([de[...], dl[...]], axis=0).astype(F32)
    top = (a0[...].astype(F32) + a1[...].astype(F32)) + (up + down)
    low = b0[...].astype(F32) + b1[...].astype(F32)
    both = jnp.concatenate([top, low], axis=0) * gain_ref[...]
    grad_ref[...] = both.T
    square = jnp.sum((both * both).reshape(128, 8, 128), axis=0)

    @pl.when(step == 0)
    def _():
        sq_ref[...] = square

    @pl.when(step > 0)
    def _():
        sq_ref[...] += square


def total(parts, gain_row, weight):
    return pl.pallas_call(
        total_kernel,
        grid=(4,),
        in_specs=[pl.BlockSpec((p.shape[0], 128), lambda t: (0, t)) for p in parts]
        + [pl.BlockSpec((1, 128), lambda t: (0, t)), pl.BlockSpec((None, 512, 256), lambda t: (0, 0, t))],
        out_specs=[
            pl.BlockSpec((128, 1024), lambda t: (t, 0)),
            pl.BlockSpec((8, 128), lambda t: (0, 0)),
            pl.BlockSpec((512 - early_rows, 256), lambda t: (0, t)),
        ],
        out_shape=[sds((512, 1024), F32), sds((8, 128), F32), sds((512 - early_rows, 1024), BF16)],
        compiler_params=params(60),
        cost_estimate=cost(5e6, 5e6),
        name="total",
    )(*parts, gain_row, weight)


def adam_kernel(table_ref, sq_ref, grad_ref, m_ref, v_ref, w_ref, first_ref, second_ref, *rest):
    outs, new_ref = rest[:-1], rest[-1]
    step = pl.program_id(0)
    squares = jnp.sum(sq_ref[...], axis=1, keepdims=True)
    squares = jnp.sum(squares, axis=0, keepdims=True)
    factor = jnp.minimum(1.0, clip_limit / jnp.sqrt(squares))
    clipped = grad_ref[...] * factor
    first = first_decay * m_ref[...] + (1.0 - first_decay) * clipped
    second = second_decay * v_ref[...] + (1.0 - second_decay) * clipped * clipped
    first_ref[...] = first
    second_ref[...] = second
    new = w_ref[...].astype(F32) - inner_rate * first / (jnp.sqrt(second) + adam_eps)
    new_ref[...] = new.astype(BF16)
    for k, out_ref in enumerate(outs):

        @pl.when(step == k)
        def _(out_ref=out_ref):
            for dx in range(2):
                out_ref[dx] = new_ref[:, pl.ds(pl.multiple_of((table_ref[4] ^ dx) * 128, 128), 128)]


def adam(table, sq, grad, first_in, second_in, weight):
    column = pl.BlockSpec((512, 256), lambda t, tab: (0, tab[t]))
    lead = pl.BlockSpec((None, 512, 256), lambda t, tab: (0, 0, tab[t]))
    return pl.pallas_call(
        adam_kernel,
        grid_spec=pltpu.PrefetchScalarGridSpec(
            num_scalar_prefetch=1,
            grid=(4,),
            in_specs=[pl.BlockSpec((8, 128), lambda t, tab: (0, 0)), column, lead, lead, lead],
            out_specs=[lead, lead] + [pl.BlockSpec((2, 512, 128), lambda t, tab: (0, 0, 0)) for k in range(4)],
            scratch_shapes=[pltpu.VMEM((512, 256), BF16)],
        ),
        out_shape=[sds((1, 512, 1024), F32)] * 2 + [sds((2, 512, 128), BF16)] * 4,
        compiler_params=params(60),
        cost_estimate=cost(2e7, 12e6),
        name="adam",
    )(table, sq, grad, first_in, second_in, weight)


def place_kernel(table_ref, *refs):
    step = pl.program_id(0)
    for k, in_ref in enumerate(refs[:-1]):

        @pl.when(step == k)
        def _(in_ref=in_ref):
            for dx in range(2):
                refs[-1][:, pl.ds(pl.multiple_of((table_ref[4] ^ dx) * 128, 128), 128)] = in_ref[dx]


def place_columns(table, parts):
    return pl.pallas_call(
        place_kernel,
        grid_spec=pltpu.PrefetchScalarGridSpec(
            num_scalar_prefetch=1,
            grid=(4,),
            in_specs=[pl.BlockSpec((2, 512, 128), lambda t, tab: (0, 0, 0)) for k in range(4)],
            out_specs=pl.BlockSpec((512, 256), lambda t, tab: (0, tab[t])),
        ),
        out_shape=sds((512, 1024), BF16),
        compiler_params=params(60),
        cost_estimate=cost(1e6, 2e6),
        name="place",
    )(table, *parts)


def input_kernel(core_ref, cp_ref, inv_ref, gain_ref, xk_ref, xs_ref, ek_ref, es_ref, lk_ref, ls_ref, out_ref, q_ref, m_ref):
    step = pl.program_id(0)
    core = core_ref[0]

    @pl.when(step == 0)
    def _():
        m_ref[...] = jnp.zeros_like(m_ref)

    @pl.when(step < 4)
    def _():
        m = m_ref[...]
        for sibling, (x_ref, e_ref, l_ref) in enumerate(((xk_ref, ek_ref, lk_ref), (xs_ref, es_ref, ls_ref))):
            for w_ref, low, high in ((e_ref, 0, early_rows), (l_ref, early_rows, 512)):
                size = high - low
                w = w_ref[...].reshape(2 * size, 1024)
                q = lax.dot_general(cp_ref[...], w, (((1,), (1,)), ((), ())), preferred_element_type=F32)
                for j in range(2):
                    g = 2 * step + j
                    gained = q[:, size * j : size * (j + 1)] * gain_ref[2 * g + (core ^ sibling)][:, low:high]
                    m = m + lane_sum(gained * x_ref[j, :, low:high].astype(F32))
                    q_ref[8 * sibling + g, :, low:high] = gained.astype(BF16)
        m_ref[...] = m

    @pl.when(step >= 4)
    def _():
        inv = inv_ref[:, 0:1]
        factor = jnp.sum(m_ref[...], axis=1, keepdims=True) * (inv * inv) / 8192.0
        for sibling, x_ref in enumerate((xk_ref, xs_ref)):
            for j in range(2):
                value = q_ref[8 * sibling + 2 * (step - 4) + j].astype(F32) - x_ref[j].astype(F32) * factor
                columns = pl.ds(pl.multiple_of(1024 * j + 512 * (core ^ sibling), 512), 512)
                out_ref[:, columns] = value.astype(BF16)


def input_gradient(core, xk, xs, cp, inv, gain, early, late):
    early = early.reshape(8, 2, early_rows, 1024)
    late = late.reshape(8, 2, 512 - early_rows, 1024)

    def weights(rows, flip):
        return pl.BlockSpec((2, None, rows, 1024), lambda t, c: (jnp.minimum(t, 3), c[0] ^ flip, 0, 0))

    x_spec = pl.BlockSpec((2, 320, 512), lambda t, c: (t % 4, 0, 0))
    return pl.pallas_call(
        input_kernel,
        grid_spec=pltpu.PrefetchScalarGridSpec(
            num_scalar_prefetch=1,
            grid=(8,),
            in_specs=[
                pl.BlockSpec((320, 1024), lambda t, c: (0, 0)),
                pl.BlockSpec((320, 128), lambda t, c: (0, 0)),
                pl.BlockSpec((16, 1, 512), lambda t, c: (0, 0, 0)),
                x_spec,
                x_spec,
                weights(early_rows, 0),
                weights(early_rows, 1),
                weights(512 - early_rows, 0),
                weights(512 - early_rows, 1),
            ],
            out_specs=pl.BlockSpec((None, 320, 2048), lambda t, c: (0, 0, jnp.maximum(t - 4, 0))),
            scratch_shapes=[pltpu.VMEM((16, 320, 512), BF16), pltpu.VMEM((320, 128), F32)],
        ),
        out_shape=sds((1, 320, 8192), BF16),
        compiler_params=params(60),
        cost_estimate=cost(6e9, 4e7),
        name="input_gradient",
    )(core, cp, inv, gain, xk, xs, early, early, late, late)


def add(*values):
    total_value = values[0].astype(F32)
    for value in values[1:]:
        total_value = total_value + value.astype(F32)
    return total_value.astype(BF16)


def on_device(
    hidden,
    replay_buffer,
    replay_index,
    cotangent,
    norm_gain,
    value_weight,
    adam_first,
    adam_second,
    anchor,
    outer_momentum,
):
    fsdp = lax.axis_index("fsdp")
    rep = lax.axis_index("rep")
    core, x, z = fsdp % 2, (fsdp // 2) % 2, fsdp // 4
    x_hi, y = rep % 2, rep // 2
    place = (z, x)
    columns = jnp.stack([(y + dy) % 4 for dy in range(4)] + [x_hi])
    gain_float = norm_gain.astype(F32)

    early = lax.all_gather(value_weight[0, :early_rows], "fsdp", axis=0, tiled=True)

    xk, xs, cp, inv = prep(core[None], hidden, replay_buffer, replay_index, cotangent)
    x_sib = over_core(xs)
    c_sib = over_core(cp)

    b_20, b_21, a_21, a_20 = grad_blocks(
        place, [2], [(0, 0, 0, 1), (0, 1, 0, 1), (1, 1, 0, 1), (1, 0, 0, 1)], xk, x_sib, cp, c_sib, "grad_a"
    )
    r_up = over_z(b_20[0], 1)
    r_down = over_z(b_21[0], -1)
    r_a2 = over_x(a_21[0])
    b_10, b_30, b_00, b_11, b_31, b_01, a_send, a_own = grad_blocks(
        place,
        [1, 3, 0],
        [(0, dx, step, 1) for dx in range(2) for step in range(3)] + [(1, 1, 0, 3), (1, 0, 0, 3)],
        xk, x_sib, cp, c_sib, "grad_b",
    )
    r_a = over_x(a_send)
    e_up = over_z(b_11[0], 1)
    e_down = over_z(b_30[0], -1)
    l_up = over_z(add(b_10[0], r_up), 1)
    l_down = over_z(add(b_31[0], r_down), -1)

    half = x_first // 2
    p_up = over_z(add(a_20[0, :half], r_a2[:half]), 1)
    p_down = over_z(add(a_20[0, half:], r_a2[half:]), -1)
    fe_up = over_z(add(a_own[0, half:], r_a[0, half:]), 1)
    fe_down = over_z(add(a_own[1, :half], r_a[1, :half]), -1)
    b_mine = add(b_00[0], l_up, e_down)
    b_theirs = add(b_01[0], e_up, l_down)
    r_b = over_x(b_theirs)
    fl_up = over_z(add(a_own[0, :half], r_a[0, :half], p_up), 1)
    fl_down = over_z(add(a_own[1, half:], r_a[1, half:], p_down), -1)

    gain_row = lax.dynamic_slice(gain_float, (fsdp * 512,), (512,))[None, :]
    grad, squares, late = total(
        [a_own[2], r_a[2], fe_up, fl_up, fe_down, fl_down, b_mine, r_b], gain_row, value_weight
    )
    late = lax.all_gather(late, "fsdp", axis=0, tiled=True)

    squares = squares + over_core(squares)
    squares = squares + over_x(squares)
    squares = squares + over_z(squares, 1) + over_z(squares, 2) + over_z(squares, 3)

    first, second, n_0, n_1, n_2, n_3 = adam(columns, squares, grad, adam_first, adam_second, value_weight)

    input_grad = input_gradient(core[None], xk, xs, cp, inv, gain_float.reshape(16, 1, 512), early, late)

    m_1 = over_y(n_1, 1)
    m_2 = over_y(n_2, 2)
    m_3 = over_y(n_3, 3)
    summed = n_0.astype(F32) + m_1.astype(F32) + m_2.astype(F32) + m_3.astype(F32)
    inner_total = summed[0] + over_x_hi(summed[1].astype(BF16)).astype(F32)
    outer_grad = anchor - inner_total / 8
    new_momentum = outer_beta * outer_momentum + outer_grad
    new_anchor = anchor - outer_rate * (outer_grad + outer_beta * new_momentum)
    sent = new_anchor.astype(BF16)
    sent = jnp.stack([sent, over_x_hi(sent)])
    parts = [sent, over_y(sent, 3), over_y(sent, 2), over_y(sent, 1)]
    synced_weight = place_columns(columns, parts)
    return (input_grad, first, second, synced_weight, new_momentum, new_anchor)


def solution(mesh):
    return jax.shard_map(
        on_device,
        mesh=mesh,
        in_specs=(
            P("rep", "fsdp", None),
            P("rep", "fsdp", None),
            P("rep", "fsdp"),
            P("rep", "fsdp", None),
            P(),
            P("rep", "fsdp", None),
            P("rep", "fsdp", None),
            P("rep", "fsdp", None),
            P("fsdp", "rep"),
            P("fsdp", "rep"),
        ),
        out_specs=(
            P("rep", "fsdp", None),
            P("rep", "fsdp", None),
            P("rep", "fsdp", None),
            P("fsdp", None),
            P("fsdp", "rep"),
            P("fsdp", "rep"),
        ),
        check_vma=False,
    )
```

```python
import functools

import jax
import jax.numpy as jnp
from jax import lax
from jax.experimental import pallas as pl
from jax.experimental.pallas import tpu as pltpu
from jax.sharding import PartitionSpec as P

norm_eps = 1e-05
adam_eps = 1e-08
inner_rate = 0.01
first_decay = 0.9
second_decay = 0.95
clip_limit = 1.0
outer_beta = 0.9
outer_rate = 0.7
replay_weight = 0.5

F32 = jnp.float32
BF16 = jnp.bfloat16
MIB = 1024 * 1024


def sds(shape, dtype):
    return jax.ShapeDtypeStruct(shape, dtype)


def cost(flops, size):
    return pl.CostEstimate(flops=int(flops), bytes_accessed=int(size), transcendentals=0)


def params(mib):
    return pltpu.CompilerParams(vmem_limit_bytes=mib * MIB)


def clip_index(t, start, count):
    return jnp.clip(t - start, 0, count - 1)


def over_core(value):
    return lax.ppermute(value, "fsdp", [(i, i ^ 1) for i in range(16)])


def over_x(value):
    return lax.ppermute(value, "fsdp", [(i, i ^ 2) for i in range(16)])


def over_z(value, step):
    return lax.ppermute(value, "fsdp", [(i, (i + 4 * step) % 16) for i in range(16)])


def over_x_hi(value):
    return lax.ppermute(value, "rep", [(i, i ^ 1) for i in range(8)])


def over_y(value, step):
    return lax.ppermute(value, "rep", [(i, (i + 2 * step) % 8) for i in range(8)])


def lane_sum(value):
    total = value[:, 0:128]
    for at in range(128, value.shape[1], 128):
        total = total + value[:, at : at + 128]
    return total


def prep_kernel(core_ref, index_ref, h_ref, b_ref, cot_ref, xk_ref, xs_ref, xf_ref, cp_ref, inv_ref, total_ref):
    step = pl.program_id(0)
    core = core_ref[0]
    rows = lax.broadcasted_iota(jnp.int32, (128, 64), 0)
    pick = jnp.where(rows == index_ref[...], 1.0, 0.0).astype(BF16)
    squares = jnp.zeros((320, 128), F32)
    for j in range(2):
        for flip, x_ref in ((0, xk_ref), (1, xs_ref)):
            columns = pl.ds(pl.multiple_of(1024 * j + 512 * (core ^ flip), 512), 512)
            replayed = lax.dot_general(pick, b_ref[:, columns], (((0,), (0,)), ((), ())), preferred_element_type=F32)
            fresh = h_ref[:, columns]
            x_ref[j, 0:256, :] = fresh
            x_ref[j, 256:320, :] = replayed.astype(BF16)
            fresh = fresh.astype(F32)
            squares = squares + jnp.concatenate([lane_sum(fresh * fresh), lane_sum(replayed * replayed)], axis=0)

    @pl.when(step == core_ref[1])
    def _():
        xf_ref[...] = xs_ref[...]

    @pl.when(step == 0)
    def _():
        total_ref[...] = squares

    @pl.when(step > 0)
    def _():
        total_ref[...] += squares

    @pl.when(step == 3)
    def _():
        mean = jnp.sum(total_ref[...], axis=1, keepdims=True) / 8192.0
        inv = lax.rsqrt(mean + norm_eps)
        inv_ref[...] = jnp.broadcast_to(inv, (320, 128))
        at = lax.broadcasted_iota(jnp.int32, (320, 1), 0)
        scale = inv * jnp.where(at < 256, 1.0, replay_weight)
        cp_ref[...] = (cot_ref[...].astype(F32) * scale).astype(BF16)


def prep(core, hidden, replay_buffer, replay_index, cotangent):
    return pl.pallas_call(
        prep_kernel,
        grid_spec=pltpu.PrefetchScalarGridSpec(
            num_scalar_prefetch=1,
            grid=(4,),
            in_specs=[
                pl.BlockSpec((1, 64), lambda t, c: (0, 0)),
                pl.BlockSpec((None, 256, 2048), lambda t, c: (0, 0, t)),
                pl.BlockSpec((None, 128, 2048), lambda t, c: (0, 0, t)),
                pl.BlockSpec((None, 320, 1024), lambda t, c: (0, 0, 0)),
            ],
            out_specs=[
                pl.BlockSpec((2, 320, 512), lambda t, c: (t, 0, 0)),
                pl.BlockSpec((2, 320, 512), lambda t, c: (t, 0, 0)),
                pl.BlockSpec((2, 320, 512), lambda t, c: (0, 0, 0)),
                pl.BlockSpec((320, 1024), lambda t, c: (0, 0)),
                pl.BlockSpec((320, 128), lambda t, c: (0, 0)),
            ],
            scratch_shapes=[pltpu.VMEM((320, 128), F32)],
        ),
        out_shape=[
            sds((8, 320, 512), BF16),
            sds((8, 320, 512), BF16),
            sds((2, 320, 512), BF16),
            sds((320, 1024), BF16),
            sds((320, 128), F32),
        ],
        compiler_params=params(60),
        cost_estimate=cost(2e9, 12e6),
        name="prep",
    )(core, replay_index, hidden, replay_buffer, cotangent)


x_first = 448
z_first = 1024 - x_first


def grad_kernel(plan, table_ref, xk_ref, xs_ref, c_ref, cs_ref, *rest):
    outs, (x_all, c_all) = rest[:-2], rest[-2:]
    step = pl.program_id(0)
    x = table_ref[4]

    @pl.when(step == 0)
    def _():
        c_all[:, 0:320] = c_ref[...].T
        c_all[:, 320:640] = cs_ref[...].T

    for dx in range(2):
        x_all[0:320, 512 * dx : 512 * dx + 512] = xk_ref[x ^ dx]
        x_all[320:640, 512 * dx : 512 * dx + 512] = xs_ref[x ^ dx]
    for at in range(max(start + count for _, _, start, count in plan)):

        @pl.when(step == at)
        def _(at=at):
            for low in range(2):
                rows = c_all[0:x_first, :] if low else c_all[x_first:1024, :]
                part = jnp.dot(rows, x_all[...], preferred_element_type=F32).astype(BF16)
                for out_ref, (out_low, dx, start, count) in zip(outs, plan):
                    if out_low == low and start <= at < start + count:
                        out_ref[...] = part[:, 512 * dx : 512 * dx + 512]


def grad_blocks(place, chunks, outputs, xk, xs, c, cs, name):
    z, x = place
    table = jnp.stack([(z + dz) % 4 for dz in chunks] + [jnp.int32(0)] * (4 - len(chunks)) + [x])
    x_spec = pl.BlockSpec((2, 320, 512), lambda t, tab: (tab[t], 0, 0))
    s_spec = x_spec if xs.shape[0] == 8 else pl.BlockSpec((2, 320, 512), lambda t, tab: (0, 0, 0))
    c_spec = pl.BlockSpec((320, 1024), lambda t, tab: (0, 0))
    return pl.pallas_call(
        functools.partial(grad_kernel, outputs),
        grid_spec=pltpu.PrefetchScalarGridSpec(
            num_scalar_prefetch=1,
            grid=(len(chunks),),
            in_specs=[x_spec, s_spec, c_spec, c_spec],
            out_specs=[
                pl.BlockSpec(
                    (None, x_first if low else z_first, 512), lambda t, tab, s=s, n=n: (clip_index(t, s, n), 0, 0)
                )
                for low, _, s, n in outputs
            ],
            scratch_shapes=[pltpu.VMEM((640, 1024), BF16), pltpu.VMEM((1024, 640), BF16)],
        ),
        out_shape=[sds((n, x_first if low else z_first, 512), BF16) for low, _, _, n in outputs],
        compiler_params=params(60),
        cost_estimate=cost(len(chunks) * 2 * 640 * 1024 * 1024, len(chunks) * 3.4e6),
        name=name,
    )(table, xk, xs, c, cs)


early_rows = 128


def late_kernel(w_ref, after_ref, late_ref):
    late_ref[...] = w_ref[early_rows:512, :]


def late_weights(weight, after):
    return pl.pallas_call(
        late_kernel,
        grid=(1,),
        in_specs=[pl.BlockSpec((None, 512, 1024), lambda t: (0, 0, 0)), pl.BlockSpec(memory_space=pl.ANY)],
        out_specs=pl.BlockSpec((512 - early_rows, 1024), lambda t: (0, 0)),
        out_shape=sds((512 - early_rows, 1024), BF16),
        compiler_params=params(60),
        cost_estimate=cost(0, 2e6),
        name="late_weights",
    )(weight, after)


def total_kernel(a0, a1, ue, ul, de, dl, b0, b1, gain_ref, grad_ref, sq_ref):
    step = pl.program_id(0)
    up = jnp.concatenate([ul[...], ue[...]], axis=0).astype(F32)
    down = jnp.concatenate([de[...], dl[...]], axis=0).astype(F32)
    top = (a0[...].astype(F32) + a1[...].astype(F32)) + (up + down)
    low = b0[...].astype(F32) + b1[...].astype(F32)
    both = jnp.concatenate([top, low], axis=0) * gain_ref[...]
    grad_ref[...] = both.T
    square = jnp.sum((both * both).reshape(128, 8, 128), axis=0)

    @pl.when(step == 0)
    def _():
        sq_ref[...] = square

    @pl.when(step > 0)
    def _():
        sq_ref[...] += square


def total(parts, gain_row):
    return pl.pallas_call(
        total_kernel,
        grid=(4,),
        in_specs=[pl.BlockSpec((p.shape[0], 128), lambda t: (0, t)) for p in parts]
        + [pl.BlockSpec((1, 128), lambda t: (0, t))],
        out_specs=[
            pl.BlockSpec((128, 1024), lambda t: (t, 0)),
            pl.BlockSpec((8, 128), lambda t: (0, 0)),
        ],
        out_shape=[sds((512, 1024), F32), sds((8, 128), F32)],
        compiler_params=params(60),
        cost_estimate=cost(5e6, 5e6),
        name="total",
    )(*parts, gain_row)


def adam_kernel(table_ref, sq_ref, grad_ref, m_ref, v_ref, w_ref, first_ref, second_ref, *rest):
    outs, new_ref = rest[:-1], rest[-1]
    step = pl.program_id(0)
    squares = jnp.sum(sq_ref[...], axis=1, keepdims=True)
    squares = jnp.sum(squares, axis=0, keepdims=True)
    factor = jnp.minimum(1.0, clip_limit / jnp.sqrt(squares))
    clipped = grad_ref[...] * factor
    first = first_decay * m_ref[...] + (1.0 - first_decay) * clipped
    second = second_decay * v_ref[...] + (1.0 - second_decay) * clipped * clipped
    first_ref[...] = first
    second_ref[...] = second
    root = second * lax.rsqrt(second) + adam_eps
    inverse = pl.reciprocal(root, approx=True)
    inverse = inverse * (2.0 - root * inverse)
    new = w_ref[...].astype(F32) - inner_rate * first * inverse
    new_ref[...] = new.astype(BF16)
    for k, out_ref in enumerate(outs):

        @pl.when(step == k)
        def _(out_ref=out_ref):
            for dx in range(2):
                out_ref[dx] = new_ref[:, pl.ds(pl.multiple_of((table_ref[4] ^ dx) * 128, 128), 128)]


def adam(table, sq, grad, first_in, second_in, weight):
    column = pl.BlockSpec((512, 256), lambda t, tab: (0, tab[t]))
    lead = pl.BlockSpec((None, 512, 256), lambda t, tab: (0, 0, tab[t]))
    return pl.pallas_call(
        adam_kernel,
        grid_spec=pltpu.PrefetchScalarGridSpec(
            num_scalar_prefetch=1,
            grid=(4,),
            in_specs=[pl.BlockSpec((8, 128), lambda t, tab: (0, 0)), column, lead, lead, lead],
            out_specs=[lead, lead] + [pl.BlockSpec((2, 512, 128), lambda t, tab: (0, 0, 0)) for k in range(4)],
            scratch_shapes=[pltpu.VMEM((512, 256), BF16)],
        ),
        out_shape=[sds((1, 512, 1024), F32)] * 2 + [sds((2, 512, 128), BF16)] * 4,
        compiler_params=params(60),
        cost_estimate=cost(2e7, 12e6),
        name="adam",
    )(table, sq, grad, first_in, second_in, weight)


def place_kernel(table_ref, *refs):
    step = pl.program_id(0)
    for k, in_ref in enumerate(refs[:-1]):

        @pl.when(step == k)
        def _(in_ref=in_ref):
            for dx in range(2):
                refs[-1][:, pl.ds(pl.multiple_of((table_ref[4] ^ dx) * 128, 128), 128)] = in_ref[dx]


def place_columns(table, parts):
    return pl.pallas_call(
        place_kernel,
        grid_spec=pltpu.PrefetchScalarGridSpec(
            num_scalar_prefetch=1,
            grid=(4,),
            in_specs=[pl.BlockSpec((2, 512, 128), lambda t, tab: (0, 0, 0)) for k in range(4)],
            out_specs=pl.BlockSpec((512, 256), lambda t, tab: (0, tab[t])),
        ),
        out_shape=sds((512, 1024), BF16),
        compiler_params=params(60),
        cost_estimate=cost(1e6, 2e6),
        name="place",
    )(table, *parts)


def early_kernel(core_ref, cp_ref, gain_ref, xk_ref, xs_ref, ek_ref, es_ref, q_ref, m_ref):
    step = pl.program_id(0)
    core = core_ref[0]
    m = jnp.zeros((320, 128), F32)
    for sibling, (x_ref, e_ref) in enumerate(((xk_ref, ek_ref), (xs_ref, es_ref))):
        w = e_ref[...].reshape(4 * early_rows, 1024)
        q = lax.dot_general(cp_ref[...], w, (((1,), (1,)), ((), ())), preferred_element_type=F32)
        for j in range(4):
            gain = gain_ref[2 * (4 * step + j) + (core ^ sibling)][:, 0:early_rows]
            gained = q[:, early_rows * j : early_rows * (j + 1)] * gain
            m = m + lane_sum(gained * x_ref[j].astype(F32))
            q_ref[sibling, j] = gained.astype(BF16)

    @pl.when(step == 0)
    def _():
        m_ref[...] = m

    @pl.when(step > 0)
    def _():
        m_ref[...] += m


def early_product(core, xk, xs, cp, gain, early):
    early = early.reshape(8, 2, early_rows, 1024)

    def weights(flip):
        return pl.BlockSpec((4, None, early_rows, 1024), lambda t, c: (t, c[0] ^ flip, 0, 0))

    x_spec = pl.BlockSpec((4, 320, early_rows), lambda t, c: (t, 0, 0))
    return pl.pallas_call(
        early_kernel,
        grid_spec=pltpu.PrefetchScalarGridSpec(
            num_scalar_prefetch=1,
            grid=(2,),
            in_specs=[
                pl.BlockSpec((320, 1024), lambda t, c: (0, 0)),
                pl.BlockSpec((16, 1, 512), lambda t, c: (0, 0, 0)),
                x_spec,
                x_spec,
                weights(0),
                weights(1),
            ],
            out_specs=[
                pl.BlockSpec((2, 4, 320, early_rows), lambda t, c: (0, t, 0, 0)),
                pl.BlockSpec((320, 128), lambda t, c: (0, 0)),
            ],
        ),
        out_shape=[sds((2, 8, 320, early_rows), BF16), sds((320, 128), F32)],
        compiler_params=params(60),
        cost_estimate=cost(1.4e9, 8e6),
        name="early_product",
    )(core, cp, gain, xk, xs, early, early)


def input_kernel(core_ref, cp_ref, inv_ref, gain_ref, xk_ref, xs_ref, qe_ref, me_ref, lk_ref, ls_ref, out_ref, q_ref, m_ref):
    step = pl.program_id(0)
    core = core_ref[0]

    @pl.when(step == 0)
    def _():
        m_ref[...] = me_ref[...]

    @pl.when(step < 4)
    def _():
        m = m_ref[...]
        for sibling, (x_ref, w_ref) in enumerate(((xk_ref, lk_ref), (xs_ref, ls_ref))):
            size = 512 - early_rows
            w = w_ref[...].reshape(2 * size, 1024)
            q = lax.dot_general(cp_ref[...], w, (((1,), (1,)), ((), ())), preferred_element_type=F32)
            for j in range(2):
                g = 2 * step + j
                gained = q[:, size * j : size * (j + 1)] * gain_ref[2 * g + (core ^ sibling)][:, early_rows:512]
                m = m + lane_sum(gained * x_ref[j, :, early_rows:512].astype(F32))
                q_ref[8 * sibling + g, :, 0:early_rows] = qe_ref[sibling, j]
                q_ref[8 * sibling + g, :, early_rows:512] = gained.astype(BF16)
        m_ref[...] = m

    @pl.when(step >= 4)
    def _():
        inv = inv_ref[:, 0:1]
        factor = jnp.sum(m_ref[...], axis=1, keepdims=True) * (inv * inv) / 8192.0
        for sibling, x_ref in enumerate((xk_ref, xs_ref)):
            for j in range(2):
                value = q_ref[8 * sibling + 2 * (step - 4) + j].astype(F32) - x_ref[j].astype(F32) * factor
                columns = pl.ds(pl.multiple_of(1024 * j + 512 * (core ^ sibling), 512), 512)
                out_ref[:, columns] = value.astype(BF16)


def input_gradient(core, xk, xs, cp, inv, gain, q_early, m_early, late):
    late = late.reshape(8, 2, 512 - early_rows, 1024)

    def weights(flip):
        return pl.BlockSpec((2, None, 512 - early_rows, 1024), lambda t, c: (jnp.minimum(t, 3), c[0] ^ flip, 0, 0))

    x_spec = pl.BlockSpec((2, 320, 512), lambda t, c: (t % 4, 0, 0))
    return pl.pallas_call(
        input_kernel,
        grid_spec=pltpu.PrefetchScalarGridSpec(
            num_scalar_prefetch=1,
            grid=(8,),
            in_specs=[
                pl.BlockSpec((320, 1024), lambda t, c: (0, 0)),
                pl.BlockSpec((320, 128), lambda t, c: (0, 0)),
                pl.BlockSpec((16, 1, 512), lambda t, c: (0, 0, 0)),
                x_spec,
                x_spec,
                pl.BlockSpec((2, 2, 320, early_rows), lambda t, c: (0, jnp.minimum(t, 3), 0, 0)),
                pl.BlockSpec((320, 128), lambda t, c: (0, 0)),
                weights(0),
                weights(1),
            ],
            out_specs=pl.BlockSpec((None, 320, 2048), lambda t, c: (0, 0, jnp.maximum(t - 4, 0))),
            scratch_shapes=[pltpu.VMEM((16, 320, 512), BF16), pltpu.VMEM((320, 128), F32)],
        ),
        out_shape=sds((1, 320, 8192), BF16),
        compiler_params=params(60),
        cost_estimate=cost(5e9, 3e7),
        name="input_gradient",
    )(core, cp, inv, gain, xk, xs, q_early, m_early, late, late)


def add(*values):
    total_value = values[0].astype(F32)
    for value in values[1:]:
        total_value = total_value + value.astype(F32)
    return total_value.astype(BF16)


def on_device(
    hidden,
    replay_buffer,
    replay_index,
    cotangent,
    norm_gain,
    value_weight,
    adam_first,
    adam_second,
    anchor,
    outer_momentum,
):
    fsdp = lax.axis_index("fsdp")
    rep = lax.axis_index("rep")
    core, x, z = fsdp % 2, (fsdp // 2) % 2, fsdp // 4
    x_hi, y = rep % 2, rep // 2
    place = (z, x)
    columns = jnp.stack([(y + dy) % 4 for dy in range(4)] + [x_hi])
    gain_float = norm_gain.astype(F32)

    early = lax.all_gather(value_weight[0, :early_rows], "fsdp", axis=0, tiled=True)

    xk, xs, xs_first, cp, inv = prep(jnp.stack([core, (z + 2) % 4]), hidden, replay_buffer, replay_index, cotangent)
    x_first_sib = over_core(xs_first)
    c_sib = over_core(cp)
    x_sib = over_core(xs)

    outer_1 = 1.0 - outer_rate * (1.0 + outer_beta)
    kept = outer_1 * anchor - (outer_rate * outer_beta * outer_beta) * outer_momentum
    kept = lax.optimization_barrier(kept)
    kept = jnp.stack([kept, over_x_hi(kept)])

    b_20, b_21, a_21, a_20 = grad_blocks(
        place, [2], [(0, 0, 0, 1), (0, 1, 0, 1), (1, 1, 0, 1), (1, 0, 0, 1)], xk, x_first_sib, cp, c_sib, "grad_a"
    )
    r_up = over_z(b_20[0], 1)
    r_down = over_z(b_21[0], -1)
    r_a2 = over_x(a_21[0])
    b_10, b_30, b_00, b_11, b_31, b_01, a_send, a_own = grad_blocks(
        place,
        [1, 3, 0],
        [(0, dx, step, 1) for dx in range(2) for step in range(3)] + [(1, 1, 0, 3), (1, 0, 0, 3)],
        xk, x_sib, cp, c_sib, "grad_b",
    )
    r_a = over_x(a_send)
    e_up = over_z(b_11[0], 1)
    e_down = over_z(b_30[0], -1)
    l_up = over_z(add(b_10[0], r_up), 1)
    l_down = over_z(add(b_31[0], r_down), -1)

    half = x_first // 2
    p_up = over_z(add(a_20[0, :half], r_a2[:half]), 1)
    p_down = over_z(add(a_20[0, half:], r_a2[half:]), -1)
    fe_up = over_z(add(a_own[0, half:], r_a[0, half:]), 1)
    fe_down = over_z(add(a_own[1, :half], r_a[1, :half]), -1)
    b_mine = add(b_00[0], l_up, e_down)
    b_theirs = add(b_01[0], e_up, l_down)
    r_b = over_x(b_theirs)
    fl_up = over_z(add(a_own[0, :half], r_a[0, :half], p_up), 1)
    fl_down = over_z(add(a_own[1, half:], r_a[1, half:], p_down), -1)

    gain_row = lax.dynamic_slice(gain_float, (fsdp * 512,), (512,))[None, :]
    grad, squares = total([a_own[2], r_a[2], fe_up, fl_up, fe_down, fl_down, b_mine, r_b], gain_row)
    late = lax.all_gather(late_weights(value_weight, l_up), "fsdp", axis=0, tiled=True)

    squares = squares + over_core(squares)
    squares = squares + over_x(squares)
    squares = squares + over_z(squares, 1) + over_z(squares, 2) + over_z(squares, 3)

    first, second, n_0, n_1, n_2, n_3 = adam(columns, squares, grad, adam_first, adam_second, value_weight)

    gain = gain_float.reshape(16, 1, 512)
    q_early, m_early = early_product(core[None], xk, xs, cp, gain, early)
    input_grad = input_gradient(core[None], xk, xs, cp, inv, gain, q_early, m_early, late)

    m_1 = over_y(n_1, 1)
    m_2 = over_y(n_2, 2)
    m_3 = over_y(n_3, 3)
    summed = add(n_0, m_1, m_2, m_3)
    inner_total = summed.astype(F32) + over_x_hi(summed[::-1]).astype(F32)
    sent = (kept + (1.0 - outer_1) / 8 * inner_total).astype(BF16)
    outer_grad = anchor - inner_total[0] / 8
    new_momentum = outer_beta * outer_momentum + outer_grad
    new_anchor = anchor - outer_rate * (outer_grad + outer_beta * new_momentum)
    parts = [sent, over_y(sent, 3), over_y(sent, 2), over_y(sent, 1)]
    synced_weight = place_columns(columns, parts)
    return (input_grad, first, second, synced_weight, new_momentum, new_anchor)


def solution(mesh):
    return jax.shard_map(
        on_device,
        mesh=mesh,
        in_specs=(
            P("rep", "fsdp", None),
            P("rep", "fsdp", None),
            P("rep", "fsdp"),
            P("rep", "fsdp", None),
            P(),
            P("rep", "fsdp", None),
            P("rep", "fsdp", None),
            P("rep", "fsdp", None),
            P("fsdp", "rep"),
            P("fsdp", "rep"),
        ),
        out_specs=(
            P("rep", "fsdp", None),
            P("rep", "fsdp", None),
            P("rep", "fsdp", None),
            P("fsdp", None),
            P("fsdp", "rep"),
            P("fsdp", "rep"),
        ),
        check_vma=False,
    )
```

```python
import functools

import jax
import jax.numpy as jnp
from jax import lax
from jax.experimental import pallas as pl
from jax.experimental.pallas import tpu as pltpu
from jax.sharding import PartitionSpec as P

norm_eps = 1e-05
adam_eps = 1e-08
inner_rate = 0.01
first_decay = 0.9
second_decay = 0.95
clip_limit = 1.0
outer_beta = 0.9
outer_rate = 0.7
replay_weight = 0.5

F32 = jnp.float32
BF16 = jnp.bfloat16
MIB = 1024 * 1024


def sds(shape, dtype):
    return jax.ShapeDtypeStruct(shape, dtype)


def cost(flops, size):
    return pl.CostEstimate(flops=int(flops), bytes_accessed=int(size), transcendentals=0)


def params(mib):
    return pltpu.CompilerParams(vmem_limit_bytes=mib * MIB)


def clip_index(t, start, count):
    return jnp.clip(t - start, 0, count - 1)


def over_core(value):
    return lax.ppermute(value, "fsdp", [(i, i ^ 1) for i in range(16)])


def over_x(value):
    return lax.ppermute(value, "fsdp", [(i, i ^ 2) for i in range(16)])


def over_z(value, step):
    return lax.ppermute(value, "fsdp", [(i, (i + 4 * step) % 16) for i in range(16)])


def over_x_hi(value):
    return lax.ppermute(value, "rep", [(i, i ^ 1) for i in range(8)])


def over_y(value, step):
    return lax.ppermute(value, "rep", [(i, (i + 2 * step) % 8) for i in range(8)])


def lane_sum(value):
    total = value[:, 0:128]
    for at in range(128, value.shape[1], 128):
        total = total + value[:, at : at + 128]
    return total


def prep_kernel(core_ref, index_ref, h_ref, b_ref, cot_ref, xk_ref, xs_ref, xf_ref, cp_ref, inv_ref, total_ref):
    step = pl.program_id(0)
    core = core_ref[0]
    rows = lax.broadcasted_iota(jnp.int32, (128, 64), 0)
    pick = jnp.where(rows == index_ref[...], 1.0, 0.0).astype(BF16)
    squares = jnp.zeros((320, 128), F32)
    for j in range(2):
        for flip, x_ref in ((0, xk_ref), (1, xs_ref)):
            columns = pl.ds(pl.multiple_of(1024 * j + 512 * (core ^ flip), 512), 512)
            replayed = lax.dot_general(pick, b_ref[:, columns], (((0,), (0,)), ((), ())), preferred_element_type=F32)
            fresh = h_ref[:, columns]
            x_ref[j, 0:256, :] = fresh
            x_ref[j, 256:320, :] = replayed.astype(BF16)
            fresh = fresh.astype(F32)
            squares = squares + jnp.concatenate([lane_sum(fresh * fresh), lane_sum(replayed * replayed)], axis=0)

    @pl.when(step == core_ref[1])
    def _():
        xf_ref[...] = xs_ref[...]

    @pl.when(step == 0)
    def _():
        total_ref[...] = squares

    @pl.when(step > 0)
    def _():
        total_ref[...] += squares

    @pl.when(step == 3)
    def _():
        mean = jnp.sum(total_ref[...], axis=1, keepdims=True) / 8192.0
        inv = lax.rsqrt(mean + norm_eps)
        inv_ref[...] = jnp.broadcast_to(inv, (320, 128))
        at = lax.broadcasted_iota(jnp.int32, (320, 1), 0)
        scale = inv * jnp.where(at < 256, 1.0, replay_weight)
        cp_ref[...] = (cot_ref[...].astype(F32) * scale).astype(BF16)


def prep(core, hidden, replay_buffer, replay_index, cotangent):
    return pl.pallas_call(
        prep_kernel,
        grid_spec=pltpu.PrefetchScalarGridSpec(
            num_scalar_prefetch=1,
            grid=(4,),
            in_specs=[
                pl.BlockSpec((1, 64), lambda t, c: (0, 0)),
                pl.BlockSpec((None, 256, 2048), lambda t, c: (0, 0, t)),
                pl.BlockSpec((None, 128, 2048), lambda t, c: (0, 0, t)),
                pl.BlockSpec((None, 320, 1024), lambda t, c: (0, 0, 0)),
            ],
            out_specs=[
                pl.BlockSpec((2, 320, 512), lambda t, c: (t, 0, 0)),
                pl.BlockSpec((2, 320, 512), lambda t, c: (t, 0, 0)),
                pl.BlockSpec((2, 320, 512), lambda t, c: (0, 0, 0)),
                pl.BlockSpec((320, 1024), lambda t, c: (0, 0)),
                pl.BlockSpec((320, 128), lambda t, c: (0, 0)),
            ],
            scratch_shapes=[pltpu.VMEM((320, 128), F32)],
        ),
        out_shape=[
            sds((8, 320, 512), BF16),
            sds((8, 320, 512), BF16),
            sds((2, 320, 512), BF16),
            sds((320, 1024), BF16),
            sds((320, 128), F32),
        ],
        compiler_params=params(60),
        cost_estimate=cost(2e9, 12e6),
        name="prep",
    )(core, replay_index, hidden, replay_buffer, cotangent)


x_first = 448
z_first = 1024 - x_first


def grad_kernel(plan, n_after, table_ref, xk_ref, xs_ref, c_ref, cs_ref, *rest):
    outs, (x_all, c_all) = rest[n_after:-2], rest[-2:]
    step = pl.program_id(0)
    x = table_ref[4]

    @pl.when(step == 0)
    def _():
        c_all[:, 0:320] = c_ref[...].T
        c_all[:, 320:640] = cs_ref[...].T

    for dx in range(2):
        x_all[0:320, 512 * dx : 512 * dx + 512] = xk_ref[x ^ dx]
        x_all[320:640, 512 * dx : 512 * dx + 512] = xs_ref[x ^ dx]
    for at in range(max(start + count for _, _, start, count in plan)):

        @pl.when(step == at)
        def _(at=at):
            for low in range(2):
                rows = c_all[0:x_first, :] if low else c_all[x_first:1024, :]
                part = jnp.dot(rows, x_all[...], preferred_element_type=F32).astype(BF16)
                for out_ref, (out_low, dx, start, count) in zip(outs, plan):
                    if out_low == low and start <= at < start + count:
                        out_ref[...] = part[:, 512 * dx : 512 * dx + 512]


def grad_blocks(place, chunks, outputs, xk, xs, c, cs, after, name):
    z, x = place
    table = jnp.stack([(z + dz) % 4 for dz in chunks] + [jnp.int32(0)] * (4 - len(chunks)) + [x])
    x_spec = pl.BlockSpec((2, 320, 512), lambda t, tab: (tab[t], 0, 0))
    s_spec = x_spec if xs.shape[0] == 8 else pl.BlockSpec((2, 320, 512), lambda t, tab: (0, 0, 0))
    c_spec = pl.BlockSpec((320, 1024), lambda t, tab: (0, 0))
    return pl.pallas_call(
        functools.partial(grad_kernel, outputs, len(after)),
        grid_spec=pltpu.PrefetchScalarGridSpec(
            num_scalar_prefetch=1,
            grid=(len(chunks),),
            in_specs=[x_spec, s_spec, c_spec, c_spec] + [pl.BlockSpec(memory_space=pl.ANY)] * len(after),
            out_specs=[
                pl.BlockSpec(
                    (None, x_first if low else z_first, 512), lambda t, tab, s=s, n=n: (clip_index(t, s, n), 0, 0)
                )
                for low, _, s, n in outputs
            ],
            scratch_shapes=[pltpu.VMEM((640, 1024), BF16), pltpu.VMEM((1024, 640), BF16)],
        ),
        out_shape=[sds((n, x_first if low else z_first, 512), BF16) for low, _, _, n in outputs],
        compiler_params=params(60),
        cost_estimate=cost(len(chunks) * 2 * 640 * 1024 * 1024, len(chunks) * 3.4e6),
        name=name,
    )(table, xk, xs, c, cs, *after)


early_rows = 128


def late_kernel(w_ref, *rest):
    rest[-1][...] = w_ref[early_rows:512, :]


def late_weights(weight, after):
    return pl.pallas_call(
        late_kernel,
        grid=(1,),
        in_specs=[pl.BlockSpec((None, 512, 1024), lambda t: (0, 0, 0))] + [pl.BlockSpec(memory_space=pl.ANY)] * len(after),
        out_specs=pl.BlockSpec((512 - early_rows, 1024), lambda t: (0, 0)),
        out_shape=sds((512 - early_rows, 1024), BF16),
        compiler_params=params(60),
        cost_estimate=cost(0, 2e6),
        name="late_weights",
    )(weight, *after)


def total_kernel(a0, a1, t1, t2, t3, b0, b1, gain_ref, after_ref, grad_ref, sq_ref):
    step = pl.program_id(0)
    top = a0[...].astype(F32) + a1[...].astype(F32)
    top = top + t1[...].astype(F32) + t2[...].astype(F32) + t3[...].astype(F32)
    low = b0[...].astype(F32) + b1[...].astype(F32)
    both = jnp.concatenate([top, low], axis=0) * gain_ref[...]
    grad_ref[...] = both.T
    square = jnp.sum(lane_sum(both * both).reshape(128, 8, 128), axis=0)

    @pl.when(step == 0)
    def _():
        sq_ref[...] = square

    @pl.when(step > 0)
    def _():
        sq_ref[...] += square


def total(parts, gain_row, after):
    return pl.pallas_call(
        total_kernel,
        grid=(2,),
        in_specs=[pl.BlockSpec((p.shape[0], 256), lambda t: (0, t)) for p in parts]
        + [pl.BlockSpec((1, 256), lambda t: (0, t))]
        + [pl.BlockSpec(memory_space=pl.ANY)] * len(after),
        out_specs=[
            pl.BlockSpec((256, 1024), lambda t: (t, 0)),
            pl.BlockSpec((8, 128), lambda t: (0, 0)),
        ],
        out_shape=[sds((512, 1024), F32), sds((8, 128), F32)],
        compiler_params=params(60),
        cost_estimate=cost(5e6, 5e6),
        name="total",
    )(*parts, gain_row, *after)


def adam_kernel(table_ref, sq_ref, grad_ref, m_ref, v_ref, w_ref, first_ref, second_ref, *rest):
    outs, new_ref = rest[:-1], rest[-1]
    squares = jnp.sum(sq_ref[...], axis=1, keepdims=True)
    squares = jnp.sum(squares, axis=0, keepdims=True)
    factor = jnp.minimum(1.0, clip_limit / jnp.sqrt(squares))
    clipped = grad_ref[...] * factor
    first = first_decay * m_ref[...] + (1.0 - first_decay) * clipped
    second = second_decay * v_ref[...] + (1.0 - second_decay) * clipped * clipped
    first_ref[...] = first
    second_ref[...] = second
    root = second * lax.rsqrt(second) + adam_eps
    inverse = pl.reciprocal(root, approx=True)
    inverse = inverse * (2.0 - root * inverse)
    new_ref[...] = (w_ref[...].astype(F32) - inner_rate * first * inverse).astype(BF16)
    for k, out_ref in enumerate(outs):
        for dx in range(2):
            column = pl.multiple_of((2 * table_ref[k] + (table_ref[4] ^ dx)) * 128, 128)
            out_ref[dx] = new_ref[:, pl.ds(column, 128)]


def adam(table, sq, grad, first_in, second_in, weight):
    rows = pl.BlockSpec((128, 1024), lambda t, tab: (t, 0))
    lead = pl.BlockSpec((None, 128, 1024), lambda t, tab: (0, t, 0))
    return pl.pallas_call(
        adam_kernel,
        grid_spec=pltpu.PrefetchScalarGridSpec(
            num_scalar_prefetch=1,
            grid=(4,),
            in_specs=[pl.BlockSpec((8, 128), lambda t, tab: (0, 0)), rows, lead, lead, lead],
            out_specs=[lead, lead] + [pl.BlockSpec((2, 128, 128), lambda t, tab: (0, t, 0)) for k in range(4)],
            scratch_shapes=[pltpu.VMEM((128, 1024), BF16)],
        ),
        out_shape=[sds((1, 512, 1024), F32)] * 2 + [sds((2, 512, 128), BF16)] * 4,
        compiler_params=params(60),
        cost_estimate=cost(2e7, 12e6),
        name="adam",
    )(table, sq, grad, first_in, second_in, weight)


def place_kernel(table_ref, *refs):
    for k, in_ref in enumerate(refs[:-1]):
        for dx in range(2):
            column = pl.multiple_of((2 * table_ref[k] + (table_ref[4] ^ dx)) * 128, 128)
            refs[-1][:, pl.ds(column, 128)] = in_ref[dx]


def place_columns(table, parts):
    return pl.pallas_call(
        place_kernel,
        grid_spec=pltpu.PrefetchScalarGridSpec(
            num_scalar_prefetch=1,
            grid=(2,),
            in_specs=[pl.BlockSpec((2, 256, 128), lambda t, tab: (0, t, 0)) for k in range(4)],
            out_specs=pl.BlockSpec((256, 1024), lambda t, tab: (t, 0)),
        ),
        out_shape=sds((512, 1024), BF16),
        compiler_params=params(60),
        cost_estimate=cost(1e6, 2e6),
        name="place",
    )(table, *parts)


def early_kernel(core_ref, cp_ref, gain_ref, xk_ref, xs_ref, ek_ref, es_ref, q_ref, m_ref):
    step = pl.program_id(0)
    core = core_ref[0]
    m = jnp.zeros((320, 128), F32)
    for sibling, (x_ref, e_ref) in enumerate(((xk_ref, ek_ref), (xs_ref, es_ref))):
        w = e_ref[...].reshape(4 * early_rows, 1024)
        q = lax.dot_general(cp_ref[...], w, (((1,), (1,)), ((), ())), preferred_element_type=F32)
        for j in range(4):
            gain = gain_ref[2 * (4 * step + j) + (core ^ sibling)][:, 0:early_rows]
            gained = q[:, early_rows * j : early_rows * (j + 1)] * gain
            m = m + lane_sum(gained * x_ref[j].astype(F32))
            q_ref[sibling, j] = gained.astype(BF16)

    @pl.when(step == 0)
    def _():
        m_ref[...] = m

    @pl.when(step > 0)
    def _():
        m_ref[...] += m


def early_product(core, xk, xs, cp, gain, early):
    early = early.reshape(8, 2, early_rows, 1024)

    def weights(flip):
        return pl.BlockSpec((4, None, early_rows, 1024), lambda t, c: (t, c[0] ^ flip, 0, 0))

    x_spec = pl.BlockSpec((4, 320, early_rows), lambda t, c: (t, 0, 0))
    return pl.pallas_call(
        early_kernel,
        grid_spec=pltpu.PrefetchScalarGridSpec(
            num_scalar_prefetch=1,
            grid=(2,),
            in_specs=[
                pl.BlockSpec((320, 1024), lambda t, c: (0, 0)),
                pl.BlockSpec((16, 1, 512), lambda t, c: (0, 0, 0)),
                x_spec,
                x_spec,
                weights(0),
                weights(1),
            ],
            out_specs=[
                pl.BlockSpec((2, 4, 320, early_rows), lambda t, c: (0, t, 0, 0)),
                pl.BlockSpec((320, 128), lambda t, c: (0, 0)),
            ],
        ),
        out_shape=[sds((2, 8, 320, early_rows), BF16), sds((320, 128), F32)],
        compiler_params=params(60),
        cost_estimate=cost(1.4e9, 8e6),
        name="early_product",
    )(core, cp, gain, xk, xs, early, early)


def input_kernel(core_ref, cp_ref, inv_ref, gain_ref, xk_ref, xs_ref, qe_ref, me_ref, lk_ref, ls_ref, out_ref, q_ref, m_ref):
    step = pl.program_id(0)
    core = core_ref[0]

    @pl.when(step == 0)
    def _():
        m_ref[...] = me_ref[...]

    @pl.when(step < 4)
    def _():
        m = m_ref[...]
        for sibling, (x_ref, w_ref) in enumerate(((xk_ref, lk_ref), (xs_ref, ls_ref))):
            size = 512 - early_rows
            w = w_ref[...].reshape(2 * size, 1024)
            q = lax.dot_general(cp_ref[...], w, (((1,), (1,)), ((), ())), preferred_element_type=F32)
            for j in range(2):
                g = 2 * step + j
                gained = q[:, size * j : size * (j + 1)] * gain_ref[2 * g + (core ^ sibling)][:, early_rows:512]
                m = m + lane_sum(gained * x_ref[j, :, early_rows:512].astype(F32))
                q_ref[8 * sibling + g, :, 0:early_rows] = qe_ref[sibling, j]
                q_ref[8 * sibling + g, :, early_rows:512] = gained.astype(BF16)
        m_ref[...] = m

    @pl.when(step >= 4)
    def _():
        inv = inv_ref[:, 0:1]
        factor = jnp.sum(m_ref[...], axis=1, keepdims=True) * (inv * inv) / 8192.0
        for sibling, x_ref in enumerate((xk_ref, xs_ref)):
            for j in range(2):
                value = q_ref[8 * sibling + 2 * (step - 4) + j].astype(F32) - x_ref[j].astype(F32) * factor
                columns = pl.ds(pl.multiple_of(1024 * j + 512 * (core ^ sibling), 512), 512)
                out_ref[:, columns] = value.astype(BF16)


def input_gradient(core, xk, xs, cp, inv, gain, q_early, m_early, late):
    late = late.reshape(8, 2, 512 - early_rows, 1024)

    def weights(flip):
        return pl.BlockSpec((2, None, 512 - early_rows, 1024), lambda t, c: (jnp.minimum(t, 3), c[0] ^ flip, 0, 0))

    x_spec = pl.BlockSpec((2, 320, 512), lambda t, c: (t % 4, 0, 0))
    return pl.pallas_call(
        input_kernel,
        grid_spec=pltpu.PrefetchScalarGridSpec(
            num_scalar_prefetch=1,
            grid=(8,),
            in_specs=[
                pl.BlockSpec((320, 1024), lambda t, c: (0, 0)),
                pl.BlockSpec((320, 128), lambda t, c: (0, 0)),
                pl.BlockSpec((16, 1, 512), lambda t, c: (0, 0, 0)),
                x_spec,
                x_spec,
                pl.BlockSpec((2, 2, 320, early_rows), lambda t, c: (0, jnp.minimum(t, 3), 0, 0)),
                pl.BlockSpec((320, 128), lambda t, c: (0, 0)),
                weights(0),
                weights(1),
            ],
            out_specs=pl.BlockSpec((None, 320, 2048), lambda t, c: (0, 0, jnp.maximum(t - 4, 0))),
            scratch_shapes=[pltpu.VMEM((16, 320, 512), BF16), pltpu.VMEM((320, 128), F32)],
        ),
        out_shape=sds((1, 320, 8192), BF16),
        compiler_params=params(60),
        cost_estimate=cost(5e9, 3e7),
        name="input_gradient",
    )(core, cp, inv, gain, xk, xs, q_early, m_early, late, late)


def add(*values):
    total_value = values[0].astype(F32)
    for value in values[1:]:
        total_value = total_value + value.astype(F32)
    return total_value.astype(BF16)


def on_device(
    hidden,
    replay_buffer,
    replay_index,
    cotangent,
    norm_gain,
    value_weight,
    adam_first,
    adam_second,
    anchor,
    outer_momentum,
):
    fsdp = lax.axis_index("fsdp")
    rep = lax.axis_index("rep")
    core, x, z = fsdp % 2, (fsdp // 2) % 2, fsdp // 4
    x_hi, y = rep % 2, rep // 2
    place = (z, x)
    columns = jnp.stack([(y + dy) % 4 for dy in range(4)] + [x_hi])
    gain_float = norm_gain.astype(F32)

    early = lax.all_gather(value_weight[0, :early_rows], "fsdp", axis=0, tiled=True)

    xk, xs, xs_first, cp, inv = prep(jnp.stack([core, (z + 2) % 4]), hidden, replay_buffer, replay_index, cotangent)
    x_first_sib = over_core(xs_first)
    c_sib = over_core(cp)
    x_sib = over_core(xs)

    outer_1 = 1.0 - outer_rate * (1.0 + outer_beta)
    kept = outer_1 * anchor - (outer_rate * outer_beta * outer_beta) * outer_momentum
    kept = lax.optimization_barrier(kept)
    kept = jnp.stack([kept, over_x_hi(kept)])

    b_20, b_21, a_21, a_20 = grad_blocks(
        place, [2], [(0, 0, 0, 1), (0, 1, 0, 1), (1, 1, 0, 1), (1, 0, 0, 1)], xk, x_first_sib, cp, c_sib, [], "grad_a"
    )
    r_up = over_z(b_20[0], 1)
    r_down = over_z(b_21[0], -1)
    r_a2 = over_x(a_21[0])
    b_10, b_30, b_00, b_11, b_31, b_01, a_send, a_own = grad_blocks(
        place,
        [1, 3, 0],
        [(0, dx, step, 1) for dx in range(2) for step in range(3)] + [(1, 1, 0, 3), (1, 0, 0, 3)],
        xk, x_sib, cp, c_sib, [kept, b_20], "grad_b",
    )
    r_a = over_x(a_send)
    e_up = over_z(b_11[0], 1)
    e_down = over_z(b_30[0], -1)
    l_up = over_z(add(b_10[0], r_up), 1)
    l_down = over_z(add(b_31[0], r_down), -1)

    s_2 = add(a_20[0], r_a2)
    t_2 = over_z(s_2, 2)
    s_1 = add(a_own[0], r_a[0])
    s_3 = add(a_own[1], r_a[1])
    t_1 = over_z(s_1, 1)
    t_3 = over_z(s_3, -1)
    b_mine = add(b_00[0], l_up, e_down)
    b_theirs = add(b_01[0], e_up, l_down)
    r_b = over_x(b_theirs)

    gain_row = lax.dynamic_slice(gain_float, (fsdp * 512,), (512,))[None, :]
    gain = gain_float.reshape(16, 1, 512)
    q_early, m_early = early_product(core[None], xk, xs, cp, gain, early)
    grad, squares = total([a_own[2], r_a[2], t_1, t_2, t_3, b_mine, r_b], gain_row, [q_early])
    late = lax.all_gather(late_weights(value_weight, [b_theirs, b_mine, s_1, s_2, s_3]), "fsdp", axis=0, tiled=True)

    squares = squares + over_core(squares)
    squares = squares + over_x(squares)
    squares = squares + over_z(squares, 1) + over_z(squares, 2) + over_z(squares, 3)

    first, second, n_0, n_1, n_2, n_3 = adam(columns, squares, grad, adam_first, adam_second, value_weight)

    input_grad = input_gradient(core[None], xk, xs, cp, inv, gain, q_early, m_early, late)

    m_1 = over_y(n_1, 1)
    m_2 = over_y(n_2, 2)
    m_3 = over_y(n_3, 3)
    summed = add(n_0, m_1, m_2, m_3)
    inner_total = summed.astype(F32) + over_x_hi(summed[::-1]).astype(F32)
    sent = (kept + (1.0 - outer_1) / 8 * inner_total).astype(BF16)
    outer_grad = anchor - inner_total[0] / 8
    new_momentum = outer_beta * outer_momentum + outer_grad
    new_anchor = anchor - outer_rate * (outer_grad + outer_beta * new_momentum)
    parts = [sent, over_y(sent, 3), over_y(sent, 2), over_y(sent, 1)]
    synced_weight = place_columns(columns, parts)
    return (input_grad, first, second, synced_weight, new_momentum, new_anchor)


def solution(mesh):
    return jax.shard_map(
        on_device,
        mesh=mesh,
        in_specs=(
            P("rep", "fsdp", None),
            P("rep", "fsdp", None),
            P("rep", "fsdp"),
            P("rep", "fsdp", None),
            P(),
            P("rep", "fsdp", None),
            P("rep", "fsdp", None),
            P("rep", "fsdp", None),
            P("fsdp", "rep"),
            P("fsdp", "rep"),
        ),
        out_specs=(
            P("rep", "fsdp", None),
            P("rep", "fsdp", None),
            P("rep", "fsdp", None),
            P("fsdp", None),
            P("fsdp", "rep"),
            P("fsdp", "rep"),
        ),
        check_vma=False,
    )
```

```python
import functools

import jax
import jax.numpy as jnp
from jax import lax
from jax.experimental import pallas as pl
from jax.experimental.pallas import tpu as pltpu
from jax.sharding import PartitionSpec as P

norm_eps = 1e-05
adam_eps = 1e-08
inner_rate = 0.01
first_decay = 0.9
second_decay = 0.95
clip_limit = 1.0
outer_beta = 0.9
outer_rate = 0.7
replay_weight = 0.5

F32 = jnp.float32
BF16 = jnp.bfloat16
MIB = 1024 * 1024


def sds(shape, dtype):
    return jax.ShapeDtypeStruct(shape, dtype)


def cost(flops, size):
    return pl.CostEstimate(flops=int(flops), bytes_accessed=int(size), transcendentals=0)


def params(mib):
    return pltpu.CompilerParams(vmem_limit_bytes=mib * MIB)


def clip_index(t, start, count):
    return jnp.clip(t - start, 0, count - 1)


def over_core(value):
    return lax.ppermute(value, "fsdp", [(i, i ^ 1) for i in range(16)])


def over_x(value):
    return lax.ppermute(value, "fsdp", [(i, i ^ 2) for i in range(16)])


def over_z(value, step):
    return lax.ppermute(value, "fsdp", [(i, (i + 4 * step) % 16) for i in range(16)])


def over_x_hi(value):
    return lax.ppermute(value, "rep", [(i, i ^ 1) for i in range(8)])


def over_y(value, step):
    return lax.ppermute(value, "rep", [(i, (i + 2 * step) % 8) for i in range(8)])


def lane_sum(value):
    total = value[:, 0:128]
    for at in range(128, value.shape[1], 128):
        total = total + value[:, at : at + 128]
    return total


def prep_kernel(core_ref, index_ref, h_ref, b_ref, cot_ref, xk_ref, xs_ref, xf_ref, cp_ref, inv_ref, total_ref):
    step = pl.program_id(0)
    core = core_ref[0]
    rows = lax.broadcasted_iota(jnp.int32, (128, 64), 0)
    pick = jnp.where(rows == index_ref[...], 1.0, 0.0).astype(BF16)
    squares = jnp.zeros((320, 128), F32)
    for j in range(2):
        for flip, x_ref in ((0, xk_ref), (1, xs_ref)):
            columns = pl.ds(pl.multiple_of(1024 * j + 512 * (core ^ flip), 512), 512)
            replayed = lax.dot_general(pick, b_ref[:, columns], (((0,), (0,)), ((), ())), preferred_element_type=F32)
            fresh = h_ref[:, columns]
            x_ref[j, 0:256, :] = fresh
            x_ref[j, 256:320, :] = replayed.astype(BF16)
            fresh = fresh.astype(F32)
            squares = squares + jnp.concatenate([lane_sum(fresh * fresh), lane_sum(replayed * replayed)], axis=0)

    @pl.when(step == core_ref[1])
    def _():
        xf_ref[...] = xs_ref[...]

    @pl.when(step == 0)
    def _():
        total_ref[...] = squares

    @pl.when(step > 0)
    def _():
        total_ref[...] += squares

    @pl.when(step == 3)
    def _():
        mean = jnp.sum(total_ref[...], axis=1, keepdims=True) / 8192.0
        inv = lax.rsqrt(mean + norm_eps)
        inv_ref[...] = jnp.broadcast_to(inv, (320, 128))
        at = lax.broadcasted_iota(jnp.int32, (320, 1), 0)
        scale = inv * jnp.where(at < 256, 1.0, replay_weight)
        cp_ref[...] = (cot_ref[...].astype(F32) * scale).astype(BF16)


def prep(core, hidden, replay_buffer, replay_index, cotangent):
    return pl.pallas_call(
        prep_kernel,
        grid_spec=pltpu.PrefetchScalarGridSpec(
            num_scalar_prefetch=1,
            grid=(4,),
            in_specs=[
                pl.BlockSpec((1, 64), lambda t, c: (0, 0)),
                pl.BlockSpec((None, 256, 2048), lambda t, c: (0, 0, t)),
                pl.BlockSpec((None, 128, 2048), lambda t, c: (0, 0, t)),
                pl.BlockSpec((None, 320, 1024), lambda t, c: (0, 0, 0)),
            ],
            out_specs=[
                pl.BlockSpec((2, 320, 512), lambda t, c: (t, 0, 0)),
                pl.BlockSpec((2, 320, 512), lambda t, c: (t, 0, 0)),
                pl.BlockSpec((2, 320, 512), lambda t, c: (0, 0, 0)),
                pl.BlockSpec((320, 1024), lambda t, c: (0, 0)),
                pl.BlockSpec((320, 128), lambda t, c: (0, 0)),
            ],
            scratch_shapes=[pltpu.VMEM((320, 128), F32)],
        ),
        out_shape=[
            sds((8, 320, 512), BF16),
            sds((8, 320, 512), BF16),
            sds((2, 320, 512), BF16),
            sds((320, 1024), BF16),
            sds((320, 128), F32),
        ],
        compiler_params=params(60),
        cost_estimate=cost(2e9, 12e6),
        name="prep",
    )(core, replay_index, hidden, replay_buffer, cotangent)


x_first = 448
z_first = 1024 - x_first


def grad_kernel(plan, n_after, table_ref, xk_ref, xs_ref, c_ref, cs_ref, *rest):
    outs, (x_all, c_all) = rest[n_after:-2], rest[-2:]
    step = pl.program_id(0)
    x = table_ref[4]

    @pl.when(step == 0)
    def _():
        c_all[:, 0:320] = c_ref[...].T
        c_all[:, 320:640] = cs_ref[...].T

    for dx in range(2):
        x_all[0:320, 512 * dx : 512 * dx + 512] = xk_ref[x ^ dx]
        x_all[320:640, 512 * dx : 512 * dx + 512] = xs_ref[x ^ dx]
    for at in range(max(start + count for _, _, start, count in plan)):

        @pl.when(step == at)
        def _(at=at):
            for low in range(2):
                rows = c_all[0:x_first, :] if low else c_all[x_first:1024, :]
                part = jnp.dot(rows, x_all[...], preferred_element_type=F32).astype(BF16)
                for out_ref, (out_low, dx, start, count) in zip(outs, plan):
                    if out_low == low and start <= at < start + count:
                        out_ref[...] = part[:, 512 * dx : 512 * dx + 512]


def grad_blocks(place, chunks, outputs, xk, xs, c, cs, after, name):
    z, x = place
    table = jnp.stack([(z + dz) % 4 for dz in chunks] + [jnp.int32(0)] * (4 - len(chunks)) + [x])
    x_spec = pl.BlockSpec((2, 320, 512), lambda t, tab: (tab[t], 0, 0))
    s_spec = x_spec if xs.shape[0] == 8 else pl.BlockSpec((2, 320, 512), lambda t, tab: (0, 0, 0))
    c_spec = pl.BlockSpec((320, 1024), lambda t, tab: (0, 0))
    return pl.pallas_call(
        functools.partial(grad_kernel, outputs, len(after)),
        grid_spec=pltpu.PrefetchScalarGridSpec(
            num_scalar_prefetch=1,
            grid=(len(chunks),),
            in_specs=[x_spec, s_spec, c_spec, c_spec] + [pl.BlockSpec(memory_space=pl.ANY)] * len(after),
            out_specs=[
                pl.BlockSpec(
                    (None, x_first if low else z_first, 512), lambda t, tab, s=s, n=n: (clip_index(t, s, n), 0, 0)
                )
                for low, _, s, n in outputs
            ],
            scratch_shapes=[pltpu.VMEM((640, 1024), BF16), pltpu.VMEM((1024, 640), BF16)],
        ),
        out_shape=[sds((n, x_first if low else z_first, 512), BF16) for low, _, _, n in outputs],
        compiler_params=params(60),
        cost_estimate=cost(len(chunks) * 2 * 640 * 1024 * 1024, len(chunks) * 3.4e6),
        name=name,
    )(table, xk, xs, c, cs, *after)


early_rows = 256


def total_kernel(a0, a1, ue, ul, de, dl, b0, b1, gain_ref, w_ref, after_ref, grad_ref, sq_ref, late_ref):
    step = pl.program_id(0)
    late_ref[...] = w_ref[early_rows:512, :]
    up = jnp.concatenate([ul[...], ue[...]], axis=0).astype(F32)
    down = jnp.concatenate([de[...], dl[...]], axis=0).astype(F32)
    top = (a0[...].astype(F32) + a1[...].astype(F32)) + (up + down)
    low = b0[...].astype(F32) + b1[...].astype(F32)
    both = jnp.concatenate([top, low], axis=0) * gain_ref[...]
    grad_ref[...] = both.T
    square = jnp.sum(lane_sum(both * both).reshape(128, 8, 128), axis=0)

    @pl.when(step == 0)
    def _():
        sq_ref[...] = square

    @pl.when(step > 0)
    def _():
        sq_ref[...] += square


def total(parts, gain_row, weight, after):
    return pl.pallas_call(
        total_kernel,
        grid=(2,),
        in_specs=[pl.BlockSpec((p.shape[0], 256), lambda t: (0, t)) for p in parts]
        + [pl.BlockSpec((1, 256), lambda t: (0, t)), pl.BlockSpec((None, 512, 512), lambda t: (0, 0, t))]
        + [pl.BlockSpec(memory_space=pl.ANY)] * len(after),
        out_specs=[
            pl.BlockSpec((256, 1024), lambda t: (t, 0)),
            pl.BlockSpec((8, 128), lambda t: (0, 0)),
            pl.BlockSpec((512 - early_rows, 512), lambda t: (0, t)),
        ],
        out_shape=[sds((512, 1024), F32), sds((8, 128), F32), sds((512 - early_rows, 1024), BF16)],
        compiler_params=params(60),
        cost_estimate=cost(5e6, 5e6),
        name="total",
    )(*parts, gain_row, weight, *after)


def adam_kernel(table_ref, sq_ref, grad_ref, m_ref, v_ref, w_ref, first_ref, second_ref, *rest):
    outs, new_ref = rest[:-1], rest[-1]
    squares = jnp.sum(sq_ref[...], axis=1, keepdims=True)
    squares = jnp.sum(squares, axis=0, keepdims=True)
    factor = jnp.minimum(1.0, clip_limit / jnp.sqrt(squares))
    clipped = grad_ref[...] * factor
    first = first_decay * m_ref[...] + (1.0 - first_decay) * clipped
    second = second_decay * v_ref[...] + (1.0 - second_decay) * clipped * clipped
    first_ref[...] = first
    second_ref[...] = second
    root = second * lax.rsqrt(second) + adam_eps
    inverse = pl.reciprocal(root, approx=True)
    inverse = inverse * (2.0 - root * inverse)
    new_ref[...] = (w_ref[...].astype(F32) - inner_rate * first * inverse).astype(BF16)
    for k, out_ref in enumerate(outs):
        for dx in range(2):
            column = pl.multiple_of((2 * table_ref[k] + (table_ref[4] ^ dx)) * 128, 128)
            out_ref[dx] = new_ref[:, pl.ds(column, 128)]


def adam(table, sq, grad, first_in, second_in, weight):
    rows = pl.BlockSpec((128, 1024), lambda t, tab: (t, 0))
    lead = pl.BlockSpec((None, 128, 1024), lambda t, tab: (0, t, 0))
    return pl.pallas_call(
        adam_kernel,
        grid_spec=pltpu.PrefetchScalarGridSpec(
            num_scalar_prefetch=1,
            grid=(4,),
            in_specs=[pl.BlockSpec((8, 128), lambda t, tab: (0, 0)), rows, lead, lead, lead],
            out_specs=[lead, lead] + [pl.BlockSpec((2, 128, 128), lambda t, tab: (0, t, 0)) for k in range(4)],
            scratch_shapes=[pltpu.VMEM((128, 1024), BF16)],
        ),
        out_shape=[sds((1, 512, 1024), F32)] * 2 + [sds((2, 512, 128), BF16)] * 4,
        compiler_params=params(60),
        cost_estimate=cost(2e7, 12e6),
        name="adam",
    )(table, sq, grad, first_in, second_in, weight)


def place_kernel(table_ref, *refs):
    for k, in_ref in enumerate(refs[:4]):
        for dx in range(2):
            column = pl.multiple_of((2 * table_ref[k] + (table_ref[4] ^ dx)) * 128, 128)
            refs[-1][:, pl.ds(column, 128)] = in_ref[dx]


def place_columns(table, parts, after):
    return pl.pallas_call(
        place_kernel,
        grid_spec=pltpu.PrefetchScalarGridSpec(
            num_scalar_prefetch=1,
            grid=(2,),
            in_specs=[pl.BlockSpec((2, 256, 128), lambda t, tab: (0, t, 0)) for k in range(4)]
            + [pl.BlockSpec(memory_space=pl.ANY)],
            out_specs=pl.BlockSpec((256, 1024), lambda t, tab: (t, 0)),
        ),
        out_shape=sds((512, 1024), BF16),
        compiler_params=params(60),
        cost_estimate=cost(1e6, 2e6),
        name="place",
    )(table, *parts, after)


def early_kernel(core_ref, cp_ref, gain_ref, xk_ref, xs_ref, ek_ref, es_ref, q_ref, m_ref):
    step = pl.program_id(0)
    core = core_ref[0]
    m = jnp.zeros((320, 128), F32)
    for sibling, (x_ref, e_ref) in enumerate(((xk_ref, ek_ref), (xs_ref, es_ref))):
        w = e_ref[...].reshape(4 * early_rows, 1024)
        q = lax.dot_general(cp_ref[...], w, (((1,), (1,)), ((), ())), preferred_element_type=F32)
        for j in range(4):
            gain = gain_ref[2 * (4 * step + j) + (core ^ sibling)][:, 0:early_rows]
            gained = q[:, early_rows * j : early_rows * (j + 1)] * gain
            m = m + lane_sum(gained * x_ref[j].astype(F32))
            q_ref[sibling, j] = gained.astype(BF16)

    @pl.when(step == 0)
    def _():
        m_ref[...] = m

    @pl.when(step > 0)
    def _():
        m_ref[...] += m


def early_product(core, xk, xs, cp, gain, early):
    early = early.reshape(8, 2, early_rows, 1024)

    def weights(flip):
        return pl.BlockSpec((4, None, early_rows, 1024), lambda t, c: (t, c[0] ^ flip, 0, 0))

    x_spec = pl.BlockSpec((4, 320, early_rows), lambda t, c: (t, 0, 0))
    return pl.pallas_call(
        early_kernel,
        grid_spec=pltpu.PrefetchScalarGridSpec(
            num_scalar_prefetch=1,
            grid=(2,),
            in_specs=[
                pl.BlockSpec((320, 1024), lambda t, c: (0, 0)),
                pl.BlockSpec((16, 1, 512), lambda t, c: (0, 0, 0)),
                x_spec,
                x_spec,
                weights(0),
                weights(1),
            ],
            out_specs=[
                pl.BlockSpec((2, 4, 320, early_rows), lambda t, c: (0, t, 0, 0)),
                pl.BlockSpec((320, 128), lambda t, c: (0, 0)),
            ],
        ),
        out_shape=[sds((2, 8, 320, early_rows), BF16), sds((320, 128), F32)],
        compiler_params=params(60),
        cost_estimate=cost(1.4e9, 8e6),
        name="early_product",
    )(core, cp, gain, xk, xs, early, early)


def input_kernel(core_ref, cp_ref, inv_ref, gain_ref, xk_ref, xs_ref, qe_ref, me_ref, lk_ref, ls_ref, out_ref, end_ref, q_ref, m_ref):
    step = pl.program_id(0)
    core = core_ref[0]

    @pl.when(step == 0)
    def _():
        m_ref[...] = me_ref[...]
        end_ref[...] = me_ref[0:8, :]

    @pl.when(step < 4)
    def _():
        m = m_ref[...]
        for sibling, (x_ref, w_ref) in enumerate(((xk_ref, lk_ref), (xs_ref, ls_ref))):
            size = 512 - early_rows
            w = w_ref[...].reshape(2 * size, 1024)
            q = lax.dot_general(cp_ref[...], w, (((1,), (1,)), ((), ())), preferred_element_type=F32)
            for j in range(2):
                g = 2 * step + j
                gained = q[:, size * j : size * (j + 1)] * gain_ref[2 * g + (core ^ sibling)][:, early_rows:512]
                m = m + lane_sum(gained * x_ref[j, :, early_rows:512].astype(F32))
                q_ref[8 * sibling + g, :, 0:early_rows] = qe_ref[sibling, j]
                q_ref[8 * sibling + g, :, early_rows:512] = gained.astype(BF16)
        m_ref[...] = m

    @pl.when(step >= 4)
    def _():
        inv = inv_ref[:, 0:1]
        factor = jnp.sum(m_ref[...], axis=1, keepdims=True) * (inv * inv) / 8192.0
        for sibling, x_ref in enumerate((xk_ref, xs_ref)):
            for j in range(2):
                value = q_ref[8 * sibling + 2 * (step - 4) + j].astype(F32) - x_ref[j].astype(F32) * factor
                columns = pl.ds(pl.multiple_of(1024 * j + 512 * (core ^ sibling), 512), 512)
                out_ref[:, columns] = value.astype(BF16)


def input_gradient(core, xk, xs, cp, inv, gain, q_early, m_early, late):
    late = late.reshape(8, 2, 512 - early_rows, 1024)

    def weights(flip):
        return pl.BlockSpec((2, None, 512 - early_rows, 1024), lambda t, c: (jnp.minimum(t, 3), c[0] ^ flip, 0, 0))

    x_spec = pl.BlockSpec((2, 320, 512), lambda t, c: (t % 4, 0, 0))
    return pl.pallas_call(
        input_kernel,
        grid_spec=pltpu.PrefetchScalarGridSpec(
            num_scalar_prefetch=1,
            grid=(8,),
            in_specs=[
                pl.BlockSpec((320, 1024), lambda t, c: (0, 0)),
                pl.BlockSpec((320, 128), lambda t, c: (0, 0)),
                pl.BlockSpec((16, 1, 512), lambda t, c: (0, 0, 0)),
                x_spec,
                x_spec,
                pl.BlockSpec((2, 2, 320, early_rows), lambda t, c: (0, jnp.minimum(t, 3), 0, 0)),
                pl.BlockSpec((320, 128), lambda t, c: (0, 0)),
                weights(0),
                weights(1),
            ],
            out_specs=[
                pl.BlockSpec((None, 320, 2048), lambda t, c: (0, 0, jnp.maximum(t - 4, 0))),
                pl.BlockSpec((8, 128), lambda t, c: (0, 0)),
            ],
            scratch_shapes=[pltpu.VMEM((16, 320, 512), BF16), pltpu.VMEM((320, 128), F32)],
        ),
        out_shape=[sds((1, 320, 8192), BF16), sds((8, 128), F32)],
        compiler_params=params(60),
        cost_estimate=cost(5e9, 3e7),
        name="input_gradient",
    )(core, cp, inv, gain, xk, xs, q_early, m_early, late, late)


def add(*values):
    total_value = values[0].astype(F32)
    for value in values[1:]:
        total_value = total_value + value.astype(F32)
    return total_value.astype(BF16)


def on_device(
    hidden,
    replay_buffer,
    replay_index,
    cotangent,
    norm_gain,
    value_weight,
    adam_first,
    adam_second,
    anchor,
    outer_momentum,
):
    fsdp = lax.axis_index("fsdp")
    rep = lax.axis_index("rep")
    core, x, z = fsdp % 2, (fsdp // 2) % 2, fsdp // 4
    x_hi, y = rep % 2, rep // 2
    place = (z, x)
    columns = jnp.stack([(y + dy) % 4 for dy in range(4)] + [x_hi])
    gain_float = norm_gain.astype(F32)

    early = lax.all_gather(value_weight[0, :early_rows], "fsdp", axis=0, tiled=True)

    xk, xs, xs_first, cp, inv = prep(jnp.stack([core, (z + 2) % 4]), hidden, replay_buffer, replay_index, cotangent)
    x_first_sib = over_core(xs_first)
    c_sib = over_core(cp)
    x_sib = over_core(xs)

    outer_1 = 1.0 - outer_rate * (1.0 + outer_beta)
    kept = outer_1 * anchor - (outer_rate * outer_beta * outer_beta) * outer_momentum
    kept = lax.optimization_barrier(kept)
    kept = jnp.stack([kept, over_x_hi(kept)])

    b_20, b_21, a_21, a_20 = grad_blocks(
        place, [2], [(0, 0, 0, 1), (0, 1, 0, 1), (1, 1, 0, 1), (1, 0, 0, 1)], xk, x_first_sib, cp, c_sib, [], "grad_a"
    )
    r_up = over_z(b_20[0], 1)
    r_down = over_z(b_21[0], -1)
    r_a2 = over_x(a_21[0])
    b_10, b_30, b_00, b_11, b_31, b_01, a_send, a_own = grad_blocks(
        place,
        [1, 3, 0],
        [(0, dx, step, 1) for dx in range(2) for step in range(3)] + [(1, 1, 0, 3), (1, 0, 0, 3)],
        xk, x_sib, cp, c_sib, [kept, b_20], "grad_b",
    )
    r_a = over_x(a_send)
    e_up = over_z(b_11[0], 1)
    e_down = over_z(b_30[0], -1)
    l_up = over_z(add(b_10[0], r_up), 1)
    l_down = over_z(add(b_31[0], r_down), -1)

    half = x_first // 2
    p_up = over_z(add(a_20[0, :half], r_a2[:half]), 1)
    p_down = over_z(add(a_20[0, half:], r_a2[half:]), -1)
    fe_up = over_z(add(a_own[0, half:], r_a[0, half:]), 1)
    fe_down = over_z(add(a_own[1, :half], r_a[1, :half]), -1)
    b_mine = add(b_00[0], l_up, e_down)
    b_theirs = add(b_01[0], e_up, l_down)
    r_b = over_x(b_theirs)
    fl_up = over_z(add(a_own[0, :half], r_a[0, :half], p_up), 1)
    fl_down = over_z(add(a_own[1, half:], r_a[1, half:], p_down), -1)

    gain_row = lax.dynamic_slice(gain_float, (fsdp * 512,), (512,))[None, :]
    gain = gain_float.reshape(16, 1, 512)
    q_early, m_early = early_product(core[None], xk, xs, cp, gain, early)
    grad, squares, late = total(
        [a_own[2], r_a[2], fe_up, fl_up, fe_down, fl_down, b_mine, r_b], gain_row, value_weight, [m_early]
    )
    late = lax.all_gather(late, "fsdp", axis=0, tiled=True)

    squares = squares + over_core(squares)
    squares = squares + over_x(squares)
    squares = squares + over_z(squares, 1) + over_z(squares, 2) + over_z(squares, 3)

    first, second, n_0, n_1, n_2, n_3 = adam(columns, squares, grad, adam_first, adam_second, value_weight)

    input_grad, input_end = input_gradient(core[None], xk, xs, cp, inv, gain, q_early, m_early, late)

    m_1 = over_y(n_1, 1)
    m_2 = over_y(n_2, 2)
    m_3 = over_y(n_3, 3)
    summed = add(n_0, m_1, m_2, m_3)
    inner_total = summed.astype(F32) + over_x_hi(summed[::-1]).astype(F32)
    sent = (kept + (1.0 - outer_1) / 8 * inner_total).astype(BF16)
    outer_grad = anchor - inner_total[0] / 8
    new_momentum = outer_beta * outer_momentum + outer_grad
    new_anchor = anchor - outer_rate * (outer_grad + outer_beta * new_momentum)
    parts = [sent, over_y(sent, 3), over_y(sent, 2), over_y(sent, 1)]
    synced_weight = place_columns(columns, parts, input_end)
    return (input_grad, first, second, synced_weight, new_momentum, new_anchor)


def solution(mesh):
    return jax.shard_map(
        on_device,
        mesh=mesh,
        in_specs=(
            P("rep", "fsdp", None),
            P("rep", "fsdp", None),
            P("rep", "fsdp"),
            P("rep", "fsdp", None),
            P(),
            P("rep", "fsdp", None),
            P("rep", "fsdp", None),
            P("rep", "fsdp", None),
            P("fsdp", "rep"),
            P("fsdp", "rep"),
        ),
        out_specs=(
            P("rep", "fsdp", None),
            P("rep", "fsdp", None),
            P("rep", "fsdp", None),
            P("fsdp", None),
            P("fsdp", "rep"),
            P("fsdp", "rep"),
        ),
        check_vma=False,
    )
```

```python
import functools

import jax
import jax.numpy as jnp
from jax import lax
from jax.experimental import pallas as pl
from jax.experimental.pallas import tpu as pltpu
from jax.sharding import PartitionSpec as P

norm_eps = 1e-05
adam_eps = 1e-08
inner_rate = 0.01
first_decay = 0.9
second_decay = 0.95
clip_limit = 1.0
outer_beta = 0.9
outer_rate = 0.7
replay_weight = 0.5
outer_kept = 1.0 - outer_rate * (1.0 + outer_beta)

F32 = jnp.float32
BF16 = jnp.bfloat16
MIB = 1024 * 1024


def sds(shape, dtype):
    return jax.ShapeDtypeStruct(shape, dtype)


def cost(flops, size):
    return pl.CostEstimate(flops=int(flops), bytes_accessed=int(size), transcendentals=0)


anywhere = pl.BlockSpec(memory_space=pl.ANY)


def params(mib):
    return pltpu.CompilerParams(vmem_limit_bytes=mib * MIB)


def clip_index(t, start, count):
    return jnp.clip(t - start, 0, count - 1)


def over_core(value):
    return lax.ppermute(value, "fsdp", [(i, i ^ 1) for i in range(16)])


def over_x(value):
    return lax.ppermute(value, "fsdp", [(i, i ^ 2) for i in range(16)])


def over_z(value, step):
    return lax.ppermute(value, "fsdp", [(i, (i + 4 * step) % 16) for i in range(16)])


def over_x_hi(value):
    return lax.ppermute(value, "rep", [(i, i ^ 1) for i in range(8)])


def over_y(value, step):
    return lax.ppermute(value, "rep", [(i, (i + 2 * step) % 8) for i in range(8)])


def lane_sum(value):
    total = value[:, 0:128]
    for at in range(128, value.shape[1], 128):
        total = total + value[:, at : at + 128]
    return total


def prep_kernel(core_ref, index_ref, h_ref, b_ref, cot_ref, xk_ref, xs_ref, xf_ref, cp_ref, inv_ref, total_ref):
    step = pl.program_id(0)
    core = core_ref[0]
    rows = lax.broadcasted_iota(jnp.int32, (128, 64), 0)
    pick = jnp.where(rows == index_ref[...], 1.0, 0.0).astype(BF16)
    squares = jnp.zeros((320, 128), F32)
    for j in range(2):
        for flip, x_ref in ((0, xk_ref), (1, xs_ref)):
            columns = pl.ds(pl.multiple_of(1024 * j + 512 * (core ^ flip), 512), 512)
            replayed = lax.dot_general(pick, b_ref[:, columns], (((0,), (0,)), ((), ())), preferred_element_type=F32)
            fresh = h_ref[:, columns]
            x_ref[j, 0:256, :] = fresh
            x_ref[j, 256:320, :] = replayed.astype(BF16)
            fresh = fresh.astype(F32)
            squares = squares + jnp.concatenate([lane_sum(fresh * fresh), lane_sum(replayed * replayed)], axis=0)

    @pl.when(step == core_ref[6])
    def _():
        xf_ref[...] = xs_ref[...]

    @pl.when(step == 0)
    def _():
        total_ref[...] = squares

    @pl.when(step > 0)
    def _():
        total_ref[...] += squares

    @pl.when(step == 3)
    def _():
        mean = jnp.sum(total_ref[...], axis=1, keepdims=True) / 8192.0
        inv = lax.rsqrt(mean + norm_eps)
        inv_ref[...] = jnp.broadcast_to(inv, (320, 128))
        at = lax.broadcasted_iota(jnp.int32, (320, 1), 0)
        scale = inv * jnp.where(at < 256, 1.0, replay_weight)
        cp_ref[...] = (cot_ref[...].astype(F32) * scale).astype(BF16)


def prep(core, hidden, replay_buffer, replay_index, cotangent):
    return pl.pallas_call(
        prep_kernel,
        grid_spec=pltpu.PrefetchScalarGridSpec(
            num_scalar_prefetch=1,
            grid=(4,),
            in_specs=[
                pl.BlockSpec((1, 64), lambda t, c: (0, 0)),
                pl.BlockSpec((None, 256, 2048), lambda t, c: (0, 0, t)),
                pl.BlockSpec((None, 128, 2048), lambda t, c: (0, 0, t)),
                pl.BlockSpec((None, 320, 1024), lambda t, c: (0, 0, 0)),
            ],
            out_specs=[
                pl.BlockSpec((2, 320, 512), lambda t, c: (t, 0, 0)),
                pl.BlockSpec((2, 320, 512), lambda t, c: (t, 0, 0)),
                pl.BlockSpec((2, 320, 512), lambda t, c: (0, 0, 0)),
                pl.BlockSpec((320, 1024), lambda t, c: (0, 0)),
                pl.BlockSpec((320, 128), lambda t, c: (0, 0)),
            ],
            scratch_shapes=[pltpu.VMEM((320, 128), F32)],
        ),
        out_shape=[
            sds((8, 320, 512), BF16),
            sds((8, 320, 512), BF16),
            sds((2, 320, 512), BF16),
            sds((320, 1024), BF16),
            sds((320, 128), F32),
        ],
        compiler_params=params(60),
        cost_estimate=cost(2e9, 12e6),
        name="prep",
    )(core, replay_index, hidden, replay_buffer, cotangent)


def after_kernel(*refs):
    pass


def after(value, *tokens):
    return pl.pallas_call(
        after_kernel,
        in_specs=[anywhere] * (1 + len(tokens)),
        out_specs=anywhere,
        out_shape=sds(value.shape, value.dtype),
        input_output_aliases={0: 0},
        cost_estimate=cost(0, 0),
        name="after",
    )(value, *tokens)


x_first = 448
z_first = 1024 - x_first


def grad_kernel(plan, n_after, table_ref, xk_ref, xs_ref, c_ref, cs_ref, *rest):
    outs, (x_all, c_all) = rest[n_after:-2], rest[-2:]
    step = pl.program_id(0)
    x = table_ref[2]

    @pl.when(step == 0)
    def _():
        c_all[:, 0:320] = c_ref[...].T
        c_all[:, 320:640] = cs_ref[...].T

    for dx in range(2):
        x_all[0:320, 512 * dx : 512 * dx + 512] = xk_ref[x ^ dx]
        x_all[320:640, 512 * dx : 512 * dx + 512] = xs_ref[x ^ dx]
    for at in range(max(start + count for _, _, start, count in plan)):

        @pl.when(step == at)
        def _(at=at):
            for low in range(2):
                rows = c_all[0:x_first, :] if low else c_all[x_first:1024, :]
                part = jnp.dot(rows, x_all[...], preferred_element_type=F32).astype(BF16)
                for out_ref, (out_low, dx, start, count) in zip(outs, plan):
                    if out_low == low and start <= at < start + count:
                        out_ref[...] = part[:, 512 * dx : 512 * dx + 512]


def grad_blocks(table, chunks, outputs, xk, xs, c, cs, after, name):
    order = chunks + [0] * (3 - len(chunks))

    def at_z(t, tab):
        dz = jnp.where(t == 0, order[0], jnp.where(t == 1, order[1], order[2]))
        return (tab[4 + dz], 0, 0)

    x_spec = pl.BlockSpec((2, 320, 512), at_z)
    s_spec = x_spec if xs.shape[0] == 8 else pl.BlockSpec((2, 320, 512), lambda t, tab: (0, 0, 0))
    c_spec = pl.BlockSpec((320, 1024), lambda t, tab: (0, 0))
    return pl.pallas_call(
        functools.partial(grad_kernel, outputs, len(after)),
        grid_spec=pltpu.PrefetchScalarGridSpec(
            num_scalar_prefetch=1,
            grid=(len(chunks),),
            in_specs=[x_spec, s_spec, c_spec, c_spec] + [pl.BlockSpec(memory_space=pl.ANY)] * len(after),
            out_specs=[
                pl.BlockSpec(
                    (None, x_first if low else z_first, 512), lambda t, tab, s=s, n=n: (clip_index(t, s, n), 0, 0)
                )
                for low, _, s, n in outputs
            ],
            scratch_shapes=[pltpu.VMEM((640, 1024), BF16), pltpu.VMEM((1024, 640), BF16)],
        ),
        out_shape=[sds((n, x_first if low else z_first, 512), BF16) for low, _, _, n in outputs],
        compiler_params=params(60),
        cost_estimate=cost(len(chunks) * 2 * 640 * 1024 * 1024, len(chunks) * 3.4e6),
        name=name,
    )(table, xk, xs, c, cs, *after)


early_rows = 128


def total_kernel(table_ref, a0, a1, ue, ul, de, dl, b0, b1, gain_ref, after_ref, grad_ref, sq_ref):
    step = pl.program_id(0)
    up = jnp.concatenate([ul[...], ue[...]], axis=0).astype(F32)
    down = jnp.concatenate([de[...], dl[...]], axis=0).astype(F32)
    top = (a0[...].astype(F32) + a1[...].astype(F32)) + (up + down)
    low = b0[...].astype(F32) + b1[...].astype(F32)
    both = jnp.concatenate([top, low], axis=0) * gain_ref[...].astype(F32)
    grad_ref[...] = both.T
    square = jnp.sum(lane_sum(both * both).reshape(128, 8, 128), axis=0)

    @pl.when(step == 0)
    def _():
        sq_ref[...] = square

    @pl.when(step > 0)
    def _():
        sq_ref[...] += square


def total(table, parts, gain, after):
    specs, arrays = [], []
    for part in parts:
        if isinstance(part, tuple):
            specs.append(pl.BlockSpec((None, part[0].shape[1], 256), lambda t, tab, k=part[1]: (k, 0, t)))
            arrays.append(part[0])
        else:
            specs.append(pl.BlockSpec((part.shape[0], 256), lambda t, tab: (0, t)))
            arrays.append(part)
    return pl.pallas_call(
        total_kernel,
        grid_spec=pltpu.PrefetchScalarGridSpec(
            num_scalar_prefetch=1,
            grid=(2,),
            in_specs=specs
            + [
                pl.BlockSpec((1, 256), lambda t, tab: (0, 2 * tab[12] + t)),
                pl.BlockSpec(memory_space=pl.ANY),
            ],
            out_specs=[
                pl.BlockSpec((256, 1024), lambda t, tab: (t, 0)),
                pl.BlockSpec((8, 128), lambda t, tab: (0, 0)),
            ],
        ),
        out_shape=[sds((512, 1024), F32), sds((8, 128), F32)],
        compiler_params=params(60),
        cost_estimate=cost(5e6, 5e6),
        name="total",
    )(table, *arrays, gain, after)


def adam_kernel(table_ref, sq_ref, grad_ref, m_ref, v_ref, w_ref, first_ref, second_ref, *rest):
    outs, new_ref = rest[:-1], rest[-1]
    squares = jnp.sum(sq_ref[...], axis=1, keepdims=True)
    squares = jnp.sum(squares, axis=0, keepdims=True)
    factor = jnp.minimum(1.0, clip_limit / jnp.sqrt(squares))
    clipped = grad_ref[...] * factor
    first = first_decay * m_ref[...] + (1.0 - first_decay) * clipped
    second = second_decay * v_ref[...] + (1.0 - second_decay) * clipped * clipped
    first_ref[...] = first
    second_ref[...] = second
    root = second * lax.rsqrt(second) + adam_eps
    inverse = pl.reciprocal(root, approx=True)
    inverse = inverse * (2.0 - root * inverse)
    new_ref[...] = (w_ref[...].astype(F32) - inner_rate * first * inverse).astype(BF16)
    for k, out_ref in enumerate(outs):
        for dx in range(2):
            column = pl.multiple_of((2 * table_ref[8 + k] + (table_ref[3] ^ dx)) * 128, 128)
            out_ref[dx] = new_ref[:, pl.ds(column, 128)]


def adam(table, sq, grad, first_in, second_in, weight):
    rows = pl.BlockSpec((128, 1024), lambda t, tab: (t, 0))
    lead = pl.BlockSpec((None, 128, 1024), lambda t, tab: (0, t, 0))
    return pl.pallas_call(
        adam_kernel,
        grid_spec=pltpu.PrefetchScalarGridSpec(
            num_scalar_prefetch=1,
            grid=(4,),
            in_specs=[pl.BlockSpec((8, 128), lambda t, tab: (0, 0)), rows, lead, lead, lead],
            out_specs=[lead, lead] + [pl.BlockSpec((2, 128, 128), lambda t, tab: (0, t, 0)) for k in range(4)],
            scratch_shapes=[pltpu.VMEM((128, 1024), BF16)],
        ),
        out_shape=[sds((1, 512, 1024), F32)] * 2 + [sds((2, 512, 128), BF16)] * 4,
        compiler_params=params(60),
        cost_estimate=cost(2e7, 12e6),
        name="adam",
    )(table, sq, grad, first_in, second_in, weight)


def place_kernel(table_ref, *refs):
    for k, in_ref in enumerate(refs[:4]):
        for dx in range(2):
            column = pl.multiple_of((2 * table_ref[8 + k] + (table_ref[3] ^ dx)) * 128, 128)
            refs[-1][:, pl.ds(column, 128)] = in_ref[dx]


def place_columns(table, parts, after):
    return pl.pallas_call(
        place_kernel,
        grid_spec=pltpu.PrefetchScalarGridSpec(
            num_scalar_prefetch=1,
            grid=(2,),
            in_specs=[pl.BlockSpec((2, 256, 128), lambda t, tab: (0, t, 0)) for k in range(4)]
            + [pl.BlockSpec(memory_space=pl.ANY)],
            out_specs=pl.BlockSpec((256, 1024), lambda t, tab: (t, 0)),
        ),
        out_shape=sds((512, 1024), BF16),
        compiler_params=params(60),
        cost_estimate=cost(1e6, 2e6),
        name="place",
    )(table, *parts, after)


def early_kernel(core_ref, cp_ref, gain_ref, xk_ref, xs_ref, ek_ref, es_ref, q_ref, m_ref):
    step = pl.program_id(0)
    core = core_ref[0]
    m = jnp.zeros((320, 128), F32)
    for sibling, (x_ref, e_ref) in enumerate(((xk_ref, ek_ref), (xs_ref, es_ref))):
        w = e_ref[...].reshape(4 * early_rows, 1024)
        q = lax.dot_general(cp_ref[...], w, (((1,), (1,)), ((), ())), preferred_element_type=F32)
        for j in range(4):
            column = pl.multiple_of((2 * (4 * step + j) + (core ^ sibling)) * 512, 512)
            gain = gain_ref[:, pl.ds(column, 512)][:, 0:early_rows].astype(F32)
            gained = q[:, early_rows * j : early_rows * (j + 1)] * gain
            m = m + lane_sum(gained * x_ref[j].astype(F32))
            q_ref[sibling, j] = gained.astype(BF16)

    @pl.when(step == 0)
    def _():
        m_ref[...] = m

    @pl.when(step > 0)
    def _():
        m_ref[...] += m


def early_product(core, xk, xs, cp, gain, early):
    early = early.reshape(8, 2, early_rows, 1024)

    def weights(flip):
        return pl.BlockSpec((4, None, early_rows, 1024), lambda t, c: (t, c[0] ^ flip, 0, 0))

    x_spec = pl.BlockSpec((4, 320, early_rows), lambda t, c: (t, 0, 0))
    return pl.pallas_call(
        early_kernel,
        grid_spec=pltpu.PrefetchScalarGridSpec(
            num_scalar_prefetch=1,
            grid=(2,),
            in_specs=[
                pl.BlockSpec((320, 1024), lambda t, c: (0, 0)),
                pl.BlockSpec((1, 8192), lambda t, c: (0, 0)),
                x_spec,
                x_spec,
                weights(0),
                weights(1),
            ],
            out_specs=[
                pl.BlockSpec((2, 4, 320, early_rows), lambda t, c: (0, t, 0, 0)),
                pl.BlockSpec((320, 128), lambda t, c: (0, 0)),
            ],
        ),
        out_shape=[sds((2, 8, 320, early_rows), BF16), sds((320, 128), F32)],
        compiler_params=params(60),
        cost_estimate=cost(1.4e9, 8e6),
        name="early_product",
    )(core, cp, gain, xk, xs, early, early)


def input_kernel(core_ref, cp_ref, inv_ref, gain_ref, xk_ref, xs_ref, qe_ref, me_ref, lk_ref, ls_ref, out_ref, end_ref, q_ref, m_ref):
    step = pl.program_id(0)
    core = core_ref[0]

    @pl.when(step == 0)
    def _():
        m_ref[...] = me_ref[...]
        end_ref[...] = me_ref[0:8, :]

    @pl.when(step < 4)
    def _():
        m = m_ref[...]
        for sibling, (x_ref, w_ref) in enumerate(((xk_ref, lk_ref), (xs_ref, ls_ref))):
            size = 512 - early_rows
            w = w_ref[...].reshape(2 * size, 1024)
            q = lax.dot_general(cp_ref[...], w, (((1,), (1,)), ((), ())), preferred_element_type=F32)
            for j in range(2):
                g = 2 * step + j
                column = pl.multiple_of((2 * g + (core ^ sibling)) * 512, 512)
                gain = gain_ref[:, pl.ds(column, 512)][:, early_rows:512].astype(F32)
                gained = q[:, size * j : size * (j + 1)] * gain
                m = m + lane_sum(gained * x_ref[j, :, early_rows:512].astype(F32))
                q_ref[8 * sibling + g, :, 0:early_rows] = qe_ref[sibling, j]
                q_ref[8 * sibling + g, :, early_rows:512] = gained.astype(BF16)
        m_ref[...] = m

    @pl.when(step >= 4)
    def _():
        inv = inv_ref[:, 0:1]
        factor = jnp.sum(m_ref[...], axis=1, keepdims=True) * (inv * inv) / 8192.0
        for sibling, x_ref in enumerate((xk_ref, xs_ref)):
            for j in range(2):
                value = q_ref[8 * sibling + 2 * (step - 4) + j].astype(F32) - x_ref[j].astype(F32) * factor
                columns = pl.ds(pl.multiple_of(1024 * j + 512 * (core ^ sibling), 512), 512)
                out_ref[:, columns] = value.astype(BF16)


def input_gradient(core, xk, xs, cp, inv, gain, q_early, m_early, late):
    late = late.reshape(8, 2, 512 - early_rows, 1024)

    def weights(flip):
        return pl.BlockSpec((2, None, 512 - early_rows, 1024), lambda t, c: (jnp.minimum(t, 3), c[0] ^ flip, 0, 0))

    x_spec = pl.BlockSpec((2, 320, 512), lambda t, c: (t % 4, 0, 0))
    return pl.pallas_call(
        input_kernel,
        grid_spec=pltpu.PrefetchScalarGridSpec(
            num_scalar_prefetch=1,
            grid=(8,),
            in_specs=[
                pl.BlockSpec((320, 1024), lambda t, c: (0, 0)),
                pl.BlockSpec((320, 128), lambda t, c: (0, 0)),
                pl.BlockSpec((1, 8192), lambda t, c: (0, 0)),
                x_spec,
                x_spec,
                pl.BlockSpec((2, 2, 320, early_rows), lambda t, c: (0, jnp.minimum(t, 3), 0, 0)),
                pl.BlockSpec((320, 128), lambda t, c: (0, 0)),
                weights(0),
                weights(1),
            ],
            out_specs=[
                pl.BlockSpec((None, 320, 2048), lambda t, c: (0, 0, jnp.maximum(t - 4, 0))),
                pl.BlockSpec((8, 128), lambda t, c: (0, 0)),
            ],
            scratch_shapes=[pltpu.VMEM((16, 320, 512), BF16), pltpu.VMEM((320, 128), F32)],
        ),
        out_shape=[sds((1, 320, 8192), BF16), sds((8, 128), F32)],
        compiler_params=params(60),
        cost_estimate=cost(5e9, 3e7),
        name="input_gradient",
    )(core, cp, inv, gain, xk, xs, q_early, m_early, late, late)


def sum_kernel(a, b, c, d, *rest):
    total_value = (a[...].astype(F32) + b[...].astype(F32)) + (c[...].astype(F32) + d[...].astype(F32))
    total_value = total_value.astype(BF16)
    sum_ref, flip_ref = rest[-2:]
    sum_ref[...] = total_value
    flip_ref[0] = total_value[1]
    flip_ref[1] = total_value[0]


def sum_over_y(parts, after):
    block = pl.BlockSpec((2, 512, 128), lambda t: (0, 0, 0))
    return pl.pallas_call(
        sum_kernel,
        grid=(1,),
        in_specs=[block] * 4 + [anywhere] * len(after),
        out_specs=[block] * 2,
        out_shape=[sds((2, 512, 128), BF16)] * 2,
        compiler_params=params(60),
        cost_estimate=cost(1e6, 2e6),
        name="sum_over_y",
    )(*parts, *after)


def outer_kernel(mine, theirs, kept_ref, kept_theirs_ref, anchor_ref, momentum_ref, sent_ref, new_momentum_ref, new_anchor_ref):
    inner_total = mine[...].astype(F32) + theirs[...].astype(F32)
    sent_ref[0] = (kept_ref[...] + (1.0 - outer_kept) / 8 * inner_total[0]).astype(BF16)
    sent_ref[1] = (kept_theirs_ref[...] + (1.0 - outer_kept) / 8 * inner_total[1]).astype(BF16)
    outer_grad = anchor_ref[...] - inner_total[0] / 8
    new_momentum = outer_beta * momentum_ref[...] + outer_grad
    new_momentum_ref[...] = new_momentum
    new_anchor_ref[...] = anchor_ref[...] - outer_rate * (outer_grad + outer_beta * new_momentum)


def outer_step(mine, theirs, kept, kept_theirs, anchor, momentum):
    pair = pl.BlockSpec((2, 512, 128), lambda t: (0, 0, 0))
    one = pl.BlockSpec((512, 128), lambda t: (0, 0))
    return pl.pallas_call(
        outer_kernel,
        grid=(1,),
        in_specs=[pair, pair, one, one, one, one],
        out_specs=[pair, one, one],
        out_shape=[sds((2, 512, 128), BF16), sds((512, 128), F32), sds((512, 128), F32)],
        compiler_params=params(60),
        cost_estimate=cost(1e6, 3e6),
        name="outer_step",
    )(mine, theirs, kept, kept_theirs, anchor, momentum)


def add(*values):
    total_value = values[0].astype(F32)
    for value in values[1:]:
        total_value = total_value + value.astype(F32)
    return total_value.astype(BF16)


def on_device(
    hidden,
    replay_buffer,
    replay_index,
    cotangent,
    norm_gain,
    value_weight,
    adam_first,
    adam_second,
    anchor,
    outer_momentum,
):
    fsdp = lax.axis_index("fsdp")
    rep = lax.axis_index("rep")
    core, x, z = fsdp % 2, (fsdp // 2) % 2, fsdp // 4
    x_hi, y = rep % 2, rep // 2
    table = jnp.stack(
        [core, z, x, x_hi] + [(z + k) % 4 for k in range(4)] + [(y + k) % 4 for k in range(4)] + [fsdp]
    )
    gain = norm_gain[None]

    early = lax.all_gather(value_weight[0, :early_rows], "fsdp", axis=0, tiled=True)

    xk, xs, xs_first, cp, inv = prep(table, hidden, replay_buffer, replay_index, cotangent)
    x_first_sib = over_core(xs_first)
    c_sib = over_core(cp)
    xs = after(xs, x_first_sib, c_sib)
    x_sib = over_core(xs)

    b_20, b_21, a_21, a_20 = grad_blocks(
        table, [2], [(0, 0, 0, 1), (0, 1, 0, 1), (1, 1, 0, 1), (1, 0, 0, 1)], xk, x_first_sib, cp, c_sib, [], "grad_a"
    )
    r_up = over_z(b_20[0], 1)
    r_down = over_z(b_21[0], -1)
    r_a2 = over_x(a_21[0])
    b_10, b_30, b_00, b_11, b_31, b_01, a_send, a_own = grad_blocks(
        table,
        [1, 3, 0],
        [(0, dx, step, 1) for dx in range(2) for step in range(3)] + [(1, 1, 0, 3), (1, 0, 0, 3)],
        xk, x_sib, cp, c_sib, [b_20], "grad_b",
    )
    r_a = over_x(after(a_send, r_a2))
    e_up = over_z(after(b_11[0], r_up), 1)
    e_down = over_z(after(b_30[0], r_down), -1)
    l_up = over_z(add(b_10[0], r_up), 1)
    l_down = over_z(add(b_31[0], r_down), -1)

    half = x_first // 2
    p_up = over_z(add(a_20[0, :half], r_a2[:half]), 1)
    p_down = over_z(add(a_20[0, half:], r_a2[half:]), -1)
    fe_up = over_z(add(a_own[0, half:], r_a[0, half:]), 1)
    fe_down = over_z(add(a_own[1, :half], r_a[1, :half]), -1)
    b_mine = add(b_00[0], l_up, e_down)
    b_theirs = add(b_01[0], e_up, l_down)
    r_b = over_x(b_theirs)
    l_1 = add(a_own[0, :half], r_a[0, :half], p_up)
    l_3 = add(a_own[1, half:], r_a[1, half:], p_down)
    fl_up = over_z(l_1, 1)
    fl_down = over_z(l_3, -1)
    late = after(value_weight[0, early_rows:], b_mine, r_b, fe_up, fe_down, l_1, l_3)
    late = lax.all_gather(late, "fsdp", axis=0, tiled=True)

    q_early, m_early = early_product(table, xk, xs, cp, gain, early)
    grad, squares = total(
        table,
        [(a_own, 2), (r_a, 2), fe_up, fl_up, fe_down, fl_down, b_mine, r_b],
        gain,
        m_early,
    )
    squares = squares + over_core(squares)
    squares = squares + over_x(squares)
    squares = squares + over_z(squares, 1) + over_z(squares, 2) + over_z(squares, 3)

    first, second, n_0, n_1, n_2, n_3 = adam(table, squares, grad, adam_first, adam_second, value_weight)

    input_grad, input_end = input_gradient(table, xk, xs, cp, inv, gain, q_early, m_early, late)

    m_1 = over_y(n_1, 1)
    m_2 = over_y(n_2, 2)
    m_3 = over_y(n_3, 3)
    kept = outer_kept * anchor - (outer_rate * outer_beta * outer_beta) * outer_momentum
    kept = lax.optimization_barrier(kept)
    kept_theirs = over_x_hi(kept)
    summed, flipped = sum_over_y([n_0, m_1, m_2, m_3], [kept_theirs])
    sent, new_momentum, new_anchor = outer_step(
        summed, over_x_hi(flipped), kept, kept_theirs, anchor, outer_momentum
    )
    parts = [sent, over_y(sent, 3), over_y(sent, 2), over_y(sent, 1)]
    synced_weight = place_columns(table, parts, input_end)
    return (input_grad, first, second, synced_weight, new_momentum, new_anchor)


def solution(mesh):
    return jax.shard_map(
        on_device,
        mesh=mesh,
        in_specs=(
            P("rep", "fsdp", None),
            P("rep", "fsdp", None),
            P("rep", "fsdp"),
            P("rep", "fsdp", None),
            P(),
            P("rep", "fsdp", None),
            P("rep", "fsdp", None),
            P("rep", "fsdp", None),
            P("fsdp", "rep"),
            P("fsdp", "rep"),
        ),
        out_specs=(
            P("rep", "fsdp", None),
            P("rep", "fsdp", None),
            P("rep", "fsdp", None),
            P("fsdp", None),
            P("fsdp", "rep"),
            P("fsdp", "rep"),
        ),
        check_vma=False,
    )
```

```python
import functools

import jax
import jax.numpy as jnp
from jax import lax
from jax.experimental import pallas as pl
from jax.experimental.pallas import tpu as pltpu
from jax.sharding import PartitionSpec as P

norm_eps = 1e-05
adam_eps = 1e-08
inner_rate = 0.01
first_decay = 0.9
second_decay = 0.95
clip_limit = 1.0
outer_beta = 0.9
outer_rate = 0.7
replay_weight = 0.5
outer_kept = 1.0 - outer_rate * (1.0 + outer_beta)

F32 = jnp.float32
BF16 = jnp.bfloat16
MIB = 1024 * 1024


def sds(shape, dtype):
    return jax.ShapeDtypeStruct(shape, dtype)


def cost(flops, size):
    return pl.CostEstimate(flops=int(flops), bytes_accessed=int(size), transcendentals=0)


anywhere = pl.BlockSpec(memory_space=pl.ANY)


def params(mib):
    return pltpu.CompilerParams(vmem_limit_bytes=mib * MIB)


def clip_index(t, start, count):
    return jnp.clip(t - start, 0, count - 1)


def over_core(value):
    return lax.ppermute(value, "fsdp", [(i, i ^ 1) for i in range(16)])


def over_x(value):
    return lax.ppermute(value, "fsdp", [(i, i ^ 2) for i in range(16)])


def over_z(value, step):
    return lax.ppermute(value, "fsdp", [(i, (i + 4 * step) % 16) for i in range(16)])


def over_x_hi(value):
    return lax.ppermute(value, "rep", [(i, i ^ 1) for i in range(8)])


def over_y(value, step):
    return lax.ppermute(value, "rep", [(i, (i + 2 * step) % 8) for i in range(8)])


def lane_sum(value):
    total = value[:, 0:128]
    for at in range(128, value.shape[1], 128):
        total = total + value[:, at : at + 128]
    return total


def prep_kernel(core_ref, index_ref, h_ref, b_ref, cot_ref, xk_ref, xs_ref, xf_ref, cp_ref, inv_ref, total_ref):
    step = pl.program_id(0)
    core = core_ref[0]
    rows = lax.broadcasted_iota(jnp.int32, (128, 64), 0)
    pick = jnp.where(rows == index_ref[...], 1.0, 0.0).astype(BF16)
    squares = jnp.zeros((320, 128), F32)
    for j in range(2):
        for flip, x_ref in ((0, xk_ref), (1, xs_ref)):
            columns = pl.ds(pl.multiple_of(1024 * j + 512 * (core ^ flip), 512), 512)
            replayed = lax.dot_general(pick, b_ref[:, columns], (((0,), (0,)), ((), ())), preferred_element_type=F32)
            fresh = h_ref[:, columns]
            x_ref[j, 0:256, :] = fresh
            x_ref[j, 256:320, :] = replayed.astype(BF16)
            fresh = fresh.astype(F32)
            squares = squares + jnp.concatenate([lane_sum(fresh * fresh), lane_sum(replayed * replayed)], axis=0)

    @pl.when(step == core_ref[6])
    def _():
        xf_ref[...] = xs_ref[...]

    @pl.when(step == 0)
    def _():
        total_ref[...] = squares

    @pl.when(step > 0)
    def _():
        total_ref[...] += squares

    @pl.when(step == 3)
    def _():
        mean = jnp.sum(total_ref[...], axis=1, keepdims=True) / 8192.0
        inv = lax.rsqrt(mean + norm_eps)
        inv_ref[...] = jnp.broadcast_to(inv, (320, 128))
        at = lax.broadcasted_iota(jnp.int32, (320, 1), 0)
        scale = inv * jnp.where(at < 256, 1.0, replay_weight)
        cp_ref[...] = (cot_ref[...].astype(F32) * scale).astype(BF16)


def prep(core, hidden, replay_buffer, replay_index, cotangent):
    return pl.pallas_call(
        prep_kernel,
        grid_spec=pltpu.PrefetchScalarGridSpec(
            num_scalar_prefetch=1,
            grid=(4,),
            in_specs=[
                pl.BlockSpec((1, 64), lambda t, c: (0, 0)),
                pl.BlockSpec((None, 256, 2048), lambda t, c: (0, 0, t)),
                pl.BlockSpec((None, 128, 2048), lambda t, c: (0, 0, t)),
                pl.BlockSpec((None, 320, 1024), lambda t, c: (0, 0, 0)),
            ],
            out_specs=[
                pl.BlockSpec((2, 320, 512), lambda t, c: (t, 0, 0)),
                pl.BlockSpec((2, 320, 512), lambda t, c: (t, 0, 0)),
                pl.BlockSpec((2, 320, 512), lambda t, c: (0, 0, 0)),
                pl.BlockSpec((320, 1024), lambda t, c: (0, 0)),
                pl.BlockSpec((320, 128), lambda t, c: (0, 0)),
            ],
            scratch_shapes=[pltpu.VMEM((320, 128), F32)],
        ),
        out_shape=[
            sds((8, 320, 512), BF16),
            sds((8, 320, 512), BF16),
            sds((2, 320, 512), BF16),
            sds((320, 1024), BF16),
            sds((320, 128), F32),
        ],
        compiler_params=params(60),
        cost_estimate=cost(2e9, 12e6),
        name="prep",
    )(core, replay_index, hidden, replay_buffer, cotangent)


def after_kernel(*refs):
    pass


def after(value, *tokens):
    return pl.pallas_call(
        after_kernel,
        in_specs=[anywhere] * (1 + len(tokens)),
        out_specs=anywhere,
        out_shape=sds(value.shape, value.dtype),
        input_output_aliases={0: 0},
        cost_estimate=cost(0, 0),
        name="after",
    )(value, *tokens)


x_first = 448
z_first = 1024 - x_first


def grad_kernel(plan, n_after, table_ref, xk_ref, xs_ref, c_ref, cs_ref, *rest):
    outs, (x_all, c_all) = rest[n_after:-2], rest[-2:]
    step = pl.program_id(0)
    x = table_ref[2]

    @pl.when(step == 0)
    def _():
        c_all[:, 0:320] = c_ref[...].T
        c_all[:, 320:640] = cs_ref[...].T

    for dx in range(2):
        x_all[0:320, 512 * dx : 512 * dx + 512] = xk_ref[x ^ dx]
        x_all[320:640, 512 * dx : 512 * dx + 512] = xs_ref[x ^ dx]
    for at in range(max(start + count for _, _, start, count in plan)):

        @pl.when(step == at)
        def _(at=at):
            for low in range(2):
                rows = c_all[0:x_first, :] if low else c_all[x_first:1024, :]
                part = jnp.dot(rows, x_all[...], preferred_element_type=F32).astype(BF16)
                for out_ref, (out_low, dx, start, count) in zip(outs, plan):
                    if out_low == low and start <= at < start + count:
                        out_ref[...] = part[:, 512 * dx : 512 * dx + 512]


def grad_blocks(table, chunks, outputs, xk, xs, c, cs, after, name):
    order = chunks + [0] * (3 - len(chunks))

    def at_z(t, tab):
        dz = jnp.where(t == 0, order[0], jnp.where(t == 1, order[1], order[2]))
        return (tab[4 + dz], 0, 0)

    x_spec = pl.BlockSpec((2, 320, 512), at_z)
    s_spec = x_spec if xs.shape[0] == 8 else pl.BlockSpec((2, 320, 512), lambda t, tab: (0, 0, 0))
    c_spec = pl.BlockSpec((320, 1024), lambda t, tab: (0, 0))
    return pl.pallas_call(
        functools.partial(grad_kernel, outputs, len(after)),
        grid_spec=pltpu.PrefetchScalarGridSpec(
            num_scalar_prefetch=1,
            grid=(len(chunks),),
            in_specs=[x_spec, s_spec, c_spec, c_spec] + [pl.BlockSpec(memory_space=pl.ANY)] * len(after),
            out_specs=[
                pl.BlockSpec(
                    (None, x_first if low else z_first, 512), lambda t, tab, s=s, n=n: (clip_index(t, s, n), 0, 0)
                )
                for low, _, s, n in outputs
            ],
            scratch_shapes=[pltpu.VMEM((640, 1024), BF16), pltpu.VMEM((1024, 640), BF16)],
        ),
        out_shape=[sds((n, x_first if low else z_first, 512), BF16) for low, _, _, n in outputs],
        compiler_params=params(60),
        cost_estimate=cost(len(chunks) * 2 * 640 * 1024 * 1024, len(chunks) * 3.4e6),
        name=name,
    )(table, xk, xs, c, cs, *after)


early_rows = 256


def total_kernel(table_ref, a0, a1, ue, ul, de, dl, b0, b1, gain_ref, w_ref, after_ref, grad_ref, sq_ref, late_ref):
    step = pl.program_id(0)
    late_ref[...] = w_ref[early_rows:512, :]
    up = jnp.concatenate([ul[...], ue[...]], axis=0).astype(F32)
    down = jnp.concatenate([de[...], dl[...]], axis=0).astype(F32)
    top = (a0[...].astype(F32) + a1[...].astype(F32)) + (up + down)
    low = b0[...].astype(F32) + b1[...].astype(F32)
    both = jnp.concatenate([top, low], axis=0) * gain_ref[...].astype(F32)
    grad_ref[...] = both.T
    square = jnp.sum(lane_sum(both * both).reshape(128, 8, 128), axis=0)

    @pl.when(step == 0)
    def _():
        sq_ref[...] = square

    @pl.when(step > 0)
    def _():
        sq_ref[...] += square


def total(table, parts, gain, weight, after):
    specs, arrays = [], []
    for part in parts:
        if isinstance(part, tuple):
            specs.append(pl.BlockSpec((None, part[0].shape[1], 256), lambda t, tab, k=part[1]: (k, 0, t)))
            arrays.append(part[0])
        else:
            specs.append(pl.BlockSpec((part.shape[0], 256), lambda t, tab: (0, t)))
            arrays.append(part)
    return pl.pallas_call(
        total_kernel,
        grid_spec=pltpu.PrefetchScalarGridSpec(
            num_scalar_prefetch=1,
            grid=(2,),
            in_specs=specs
            + [
                pl.BlockSpec((1, 256), lambda t, tab: (0, 2 * tab[12] + t)),
                pl.BlockSpec((None, 512, 512), lambda t, tab: (0, 0, t)),
                pl.BlockSpec(memory_space=pl.ANY),
            ],
            out_specs=[
                pl.BlockSpec((256, 1024), lambda t, tab: (t, 0)),
                pl.BlockSpec((8, 128), lambda t, tab: (0, 0)),
                pl.BlockSpec((512 - early_rows, 512), lambda t, tab: (0, t)),
            ],
        ),
        out_shape=[sds((512, 1024), F32), sds((8, 128), F32), sds((512 - early_rows, 1024), BF16)],
        compiler_params=params(60),
        cost_estimate=cost(5e6, 5e6),
        name="total",
    )(table, *arrays, gain, weight, after)


def adam_kernel(table_ref, sq_ref, grad_ref, m_ref, v_ref, w_ref, first_ref, second_ref, *rest):
    outs, new_ref = rest[:-1], rest[-1]
    squares = jnp.sum(sq_ref[...], axis=1, keepdims=True)
    squares = jnp.sum(squares, axis=0, keepdims=True)
    factor = jnp.minimum(1.0, clip_limit / jnp.sqrt(squares))
    clipped = grad_ref[...] * factor
    first = first_decay * m_ref[...] + (1.0 - first_decay) * clipped
    second = second_decay * v_ref[...] + (1.0 - second_decay) * clipped * clipped
    first_ref[...] = first
    second_ref[...] = second
    root = second * lax.rsqrt(second) + adam_eps
    inverse = pl.reciprocal(root, approx=True)
    inverse = inverse * (2.0 - root * inverse)
    new_ref[...] = (w_ref[...].astype(F32) - inner_rate * first * inverse).astype(BF16)
    for k, out_ref in enumerate(outs):
        for dx in range(2):
            column = pl.multiple_of((2 * table_ref[8 + k] + (table_ref[3] ^ dx)) * 128, 128)
            out_ref[dx] = new_ref[:, pl.ds(column, 128)]


def adam(table, sq, grad, first_in, second_in, weight):
    rows = pl.BlockSpec((128, 1024), lambda t, tab: (t, 0))
    lead = pl.BlockSpec((None, 128, 1024), lambda t, tab: (0, t, 0))
    return pl.pallas_call(
        adam_kernel,
        grid_spec=pltpu.PrefetchScalarGridSpec(
            num_scalar_prefetch=1,
            grid=(4,),
            in_specs=[pl.BlockSpec((8, 128), lambda t, tab: (0, 0)), rows, lead, lead, lead],
            out_specs=[lead, lead] + [pl.BlockSpec((2, 128, 128), lambda t, tab: (0, t, 0)) for k in range(4)],
            scratch_shapes=[pltpu.VMEM((128, 1024), BF16)],
        ),
        out_shape=[sds((1, 512, 1024), F32)] * 2 + [sds((2, 512, 128), BF16)] * 4,
        compiler_params=params(60),
        cost_estimate=cost(2e7, 12e6),
        name="adam",
    )(table, sq, grad, first_in, second_in, weight)


def place_kernel(table_ref, *refs):
    for k, in_ref in enumerate(refs[:4]):
        for dx in range(2):
            column = pl.multiple_of((2 * table_ref[8 + k] + (table_ref[3] ^ dx)) * 128, 128)
            refs[-1][:, pl.ds(column, 128)] = in_ref[dx]


def place_columns(table, parts, after):
    return pl.pallas_call(
        place_kernel,
        grid_spec=pltpu.PrefetchScalarGridSpec(
            num_scalar_prefetch=1,
            grid=(2,),
            in_specs=[pl.BlockSpec((2, 256, 128), lambda t, tab: (0, t, 0)) for k in range(4)]
            + [pl.BlockSpec(memory_space=pl.ANY)],
            out_specs=pl.BlockSpec((256, 1024), lambda t, tab: (t, 0)),
        ),
        out_shape=sds((512, 1024), BF16),
        compiler_params=params(60),
        cost_estimate=cost(1e6, 2e6),
        name="place",
    )(table, *parts, after)


def early_kernel(core_ref, cp_ref, gain_ref, xk_ref, xs_ref, ek_ref, es_ref, q_ref, m_ref):
    step = pl.program_id(0)
    core = core_ref[0]
    m = jnp.zeros((320, 128), F32)
    for sibling, (x_ref, e_ref) in enumerate(((xk_ref, ek_ref), (xs_ref, es_ref))):
        w = e_ref[...].reshape(4 * early_rows, 1024)
        q = lax.dot_general(cp_ref[...], w, (((1,), (1,)), ((), ())), preferred_element_type=F32)
        for j in range(4):
            column = pl.multiple_of((2 * (4 * step + j) + (core ^ sibling)) * 512, 512)
            gain = gain_ref[:, pl.ds(column, 512)][:, 0:early_rows].astype(F32)
            gained = q[:, early_rows * j : early_rows * (j + 1)] * gain
            m = m + lane_sum(gained * x_ref[j].astype(F32))
            q_ref[sibling, j] = gained.astype(BF16)

    @pl.when(step == 0)
    def _():
        m_ref[...] = m

    @pl.when(step > 0)
    def _():
        m_ref[...] += m


def early_product(core, xk, xs, cp, gain, early):
    early = early.reshape(8, 2, early_rows, 1024)

    def weights(flip):
        return pl.BlockSpec((4, None, early_rows, 1024), lambda t, c: (t, c[0] ^ flip, 0, 0))

    x_spec = pl.BlockSpec((4, 320, early_rows), lambda t, c: (t, 0, 0))
    return pl.pallas_call(
        early_kernel,
        grid_spec=pltpu.PrefetchScalarGridSpec(
            num_scalar_prefetch=1,
            grid=(2,),
            in_specs=[
                pl.BlockSpec((320, 1024), lambda t, c: (0, 0)),
                pl.BlockSpec((1, 8192), lambda t, c: (0, 0)),
                x_spec,
                x_spec,
                weights(0),
                weights(1),
            ],
            out_specs=[
                pl.BlockSpec((2, 4, 320, early_rows), lambda t, c: (0, t, 0, 0)),
                pl.BlockSpec((320, 128), lambda t, c: (0, 0)),
            ],
        ),
        out_shape=[sds((2, 8, 320, early_rows), BF16), sds((320, 128), F32)],
        compiler_params=params(60),
        cost_estimate=cost(1.4e9, 8e6),
        name="early_product",
    )(core, cp, gain, xk, xs, early, early)


def input_kernel(core_ref, cp_ref, inv_ref, gain_ref, xk_ref, xs_ref, qe_ref, me_ref, lk_ref, ls_ref, out_ref, end_ref, q_ref, m_ref):
    step = pl.program_id(0)
    core = core_ref[0]

    @pl.when(step == 0)
    def _():
        m_ref[...] = me_ref[...]
        end_ref[...] = me_ref[0:8, :]

    @pl.when(step < 4)
    def _():
        m = m_ref[...]
        for sibling, (x_ref, w_ref) in enumerate(((xk_ref, lk_ref), (xs_ref, ls_ref))):
            size = 512 - early_rows
            w = w_ref[...].reshape(2 * size, 1024)
            q = lax.dot_general(cp_ref[...], w, (((1,), (1,)), ((), ())), preferred_element_type=F32)
            for j in range(2):
                g = 2 * step + j
                column = pl.multiple_of((2 * g + (core ^ sibling)) * 512, 512)
                gain = gain_ref[:, pl.ds(column, 512)][:, early_rows:512].astype(F32)
                gained = q[:, size * j : size * (j + 1)] * gain
                m = m + lane_sum(gained * x_ref[j, :, early_rows:512].astype(F32))
                q_ref[8 * sibling + g, :, 0:early_rows] = qe_ref[sibling, j]
                q_ref[8 * sibling + g, :, early_rows:512] = gained.astype(BF16)
        m_ref[...] = m

    @pl.when(step >= 4)
    def _():
        inv = inv_ref[:, 0:1]
        factor = jnp.sum(m_ref[...], axis=1, keepdims=True) * (inv * inv) / 8192.0
        for sibling, x_ref in enumerate((xk_ref, xs_ref)):
            for j in range(2):
                value = q_ref[8 * sibling + 2 * (step - 4) + j].astype(F32) - x_ref[j].astype(F32) * factor
                columns = pl.ds(pl.multiple_of(1024 * j + 512 * (core ^ sibling), 512), 512)
                out_ref[:, columns] = value.astype(BF16)


def input_gradient(core, xk, xs, cp, inv, gain, q_early, m_early, late):
    late = late.reshape(8, 2, 512 - early_rows, 1024)

    def weights(flip):
        return pl.BlockSpec((2, None, 512 - early_rows, 1024), lambda t, c: (jnp.minimum(t, 3), c[0] ^ flip, 0, 0))

    x_spec = pl.BlockSpec((2, 320, 512), lambda t, c: (t % 4, 0, 0))
    return pl.pallas_call(
        input_kernel,
        grid_spec=pltpu.PrefetchScalarGridSpec(
            num_scalar_prefetch=1,
            grid=(8,),
            in_specs=[
                pl.BlockSpec((320, 1024), lambda t, c: (0, 0)),
                pl.BlockSpec((320, 128), lambda t, c: (0, 0)),
                pl.BlockSpec((1, 8192), lambda t, c: (0, 0)),
                x_spec,
                x_spec,
                pl.BlockSpec((2, 2, 320, early_rows), lambda t, c: (0, jnp.minimum(t, 3), 0, 0)),
                pl.BlockSpec((320, 128), lambda t, c: (0, 0)),
                weights(0),
                weights(1),
            ],
            out_specs=[
                pl.BlockSpec((None, 320, 2048), lambda t, c: (0, 0, jnp.maximum(t - 4, 0))),
                pl.BlockSpec((8, 128), lambda t, c: (0, 0)),
            ],
            scratch_shapes=[pltpu.VMEM((16, 320, 512), BF16), pltpu.VMEM((320, 128), F32)],
        ),
        out_shape=[sds((1, 320, 8192), BF16), sds((8, 128), F32)],
        compiler_params=params(60),
        cost_estimate=cost(5e9, 3e7),
        name="input_gradient",
    )(core, cp, inv, gain, xk, xs, q_early, m_early, late, late)


def add(*values):
    total_value = values[0].astype(F32)
    for value in values[1:]:
        total_value = total_value + value.astype(F32)
    return total_value.astype(BF16)


def on_device(
    hidden,
    replay_buffer,
    replay_index,
    cotangent,
    norm_gain,
    value_weight,
    adam_first,
    adam_second,
    anchor,
    outer_momentum,
):
    fsdp = lax.axis_index("fsdp")
    rep = lax.axis_index("rep")
    core, x, z = fsdp % 2, (fsdp // 2) % 2, fsdp // 4
    x_hi, y = rep % 2, rep // 2
    table = jnp.stack(
        [core, z, x, x_hi] + [(z + k) % 4 for k in range(4)] + [(y + k) % 4 for k in range(4)] + [fsdp]
    )
    gain = norm_gain[None]

    early = lax.all_gather(value_weight[0, :early_rows], "fsdp", axis=0, tiled=True)

    xk, xs, xs_first, cp, inv = prep(table, hidden, replay_buffer, replay_index, cotangent)
    x_first_sib = over_core(xs_first)
    c_sib = over_core(cp)
    xs = after(xs, x_first_sib, c_sib)
    x_sib = over_core(xs)

    b_20, b_21, a_21, a_20 = grad_blocks(
        table, [2], [(0, 0, 0, 1), (0, 1, 0, 1), (1, 1, 0, 1), (1, 0, 0, 1)], xk, x_first_sib, cp, c_sib, [], "grad_a"
    )
    r_up = over_z(b_20[0], 1)
    r_down = over_z(b_21[0], -1)
    r_a2 = over_x(a_21[0])
    b_10, b_30, b_00, b_11, b_31, b_01, a_send, a_own = grad_blocks(
        table,
        [1, 3, 0],
        [(0, dx, step, 1) for dx in range(2) for step in range(3)] + [(1, 1, 0, 3), (1, 0, 0, 3)],
        xk, x_sib, cp, c_sib, [b_20], "grad_b",
    )
    r_a = over_x(after(a_send, r_a2))
    e_up = over_z(after(b_11[0], r_up), 1)
    e_down = over_z(after(b_30[0], r_down), -1)
    l_up = over_z(add(b_10[0], r_up), 1)
    l_down = over_z(add(b_31[0], r_down), -1)

    half = x_first // 2
    p_up = over_z(add(a_20[0, :half], r_a2[:half]), 1)
    p_down = over_z(add(a_20[0, half:], r_a2[half:]), -1)
    fe_up = over_z(add(a_own[0, half:], r_a[0, half:]), 1)
    fe_down = over_z(add(a_own[1, :half], r_a[1, :half]), -1)
    b_mine = add(b_00[0], l_up, e_down)
    b_theirs = add(b_01[0], e_up, l_down)
    r_b = over_x(b_theirs)
    fl_up = over_z(add(a_own[0, :half], r_a[0, :half], p_up), 1)
    fl_down = over_z(add(a_own[1, half:], r_a[1, half:], p_down), -1)

    q_early, m_early = early_product(table, xk, xs, cp, gain, early)
    grad, squares, late = total(
        table,
        [(a_own, 2), (r_a, 2), fe_up, fl_up, fe_down, fl_down, b_mine, r_b],
        gain,
        value_weight,
        m_early,
    )
    late = lax.all_gather(late, "fsdp", axis=0, tiled=True)

    squares = squares + over_core(squares)
    squares = squares + over_x(squares)
    squares = squares + over_z(squares, 1) + over_z(squares, 2) + over_z(squares, 3)

    first, second, n_0, n_1, n_2, n_3 = adam(table, squares, grad, adam_first, adam_second, value_weight)

    input_grad, input_end = input_gradient(table, xk, xs, cp, inv, gain, q_early, m_early, late)

    m_1 = over_y(n_1, 1)
    m_2 = over_y(n_2, 2)
    m_3 = over_y(n_3, 3)
    kept = outer_kept * anchor - (outer_rate * outer_beta * outer_beta) * outer_momentum
    kept = lax.optimization_barrier(kept)
    kept_theirs = over_x_hi(kept)
    kept = jnp.stack([kept, kept_theirs])
    summed = add(after(n_0, kept_theirs), m_1, m_2, m_3)
    inner_total = summed.astype(F32) + over_x_hi(summed[::-1]).astype(F32)
    sent = (kept + (1.0 - outer_kept) / 8 * inner_total).astype(BF16)
    outer_grad = anchor - inner_total[0] / 8
    new_momentum = outer_beta * outer_momentum + outer_grad
    new_anchor = anchor - outer_rate * (outer_grad + outer_beta * new_momentum)
    parts = [sent, over_y(sent, 3), over_y(sent, 2), over_y(sent, 1)]
    synced_weight = place_columns(table, parts, input_end)
    return (input_grad, first, second, synced_weight, new_momentum, new_anchor)


def solution(mesh):
    return jax.shard_map(
        on_device,
        mesh=mesh,
        in_specs=(
            P("rep", "fsdp", None),
            P("rep", "fsdp", None),
            P("rep", "fsdp"),
            P("rep", "fsdp", None),
            P(),
            P("rep", "fsdp", None),
            P("rep", "fsdp", None),
            P("rep", "fsdp", None),
            P("fsdp", "rep"),
            P("fsdp", "rep"),
        ),
        out_specs=(
            P("rep", "fsdp", None),
            P("rep", "fsdp", None),
            P("rep", "fsdp", None),
            P("fsdp", None),
            P("fsdp", "rep"),
            P("fsdp", "rep"),
        ),
        check_vma=False,
    )
```
